32 devices in a mesh: sx: 2 (over core), sy: 4 (over z), gz: 4 (over y, x).
Axes of the slice: x: 2, y: 2, z: 4, core: 2. Of those that a mesh axis runs over, the one named last changes fastest.
Arguments:
- field: float32 [8, 512, 4096], P('gz', 'sy', 'sx'), may hold values from 0.1 to 2
- bins: int32 [8, 512, 4096], P('gz', 'sy', 'sx'), may hold values from 0 to 127
- table: bfloat16 [4, 128], replicated, may hold values from 0.02 to 1, as said below
- march_order: int32 [512], P('sy'), may hold values from 0 to 1
Outputs:
- image: float32 [4, 512, 4096], P(None, ('sy', 'gz'), 'sx')
The draws below stay inside these ranges and needn't reach their ends.
Inputs may be any that keep to these rules, and one draw needn't show every extreme that they name: `table`: rows 0 to 2 lie between 0.05 and 1, row 3 between 0.02 and about 0.12.
All inputs are finite; a program needn't handle non-finite values.
Results may differ from the reference program's by a relative error of at most 0.0003.
Values sent between devices are 32-bit elements; how exact they have to be, the bound alone decides.
No kernel may reach another device: no remote copies, remote signals or barrier semaphores. Data moves between devices by JAX's collectives and lax.ppermute only.
A program may use at most 128 MiB of HBM per device.

```python
import math
import jax
import jax.numpy as jnp
from jax import lax

NBINS = 128
NX = 4096
NY = 512
NZ = 8


def draw_table(key, part):
    key = jax.random.fold_in(key, 7)
    first = jax.random.fold_in(key, 1)
    second = jax.random.fold_in(key, 2)
    colours = jax.random.uniform(first, (3, NBINS), jnp.float32, 0.05, 1.0)
    opacity = jax.random.uniform(second, (1, NBINS), jnp.float32, 0.02, 0.12)
    return jnp.concatenate([colours, opacity], 0).astype(jnp.bfloat16)


def set_ends(array, key, low, top_value):
    longest = array.shape.index(max(array.shape))
    spots = []
    for shift in (0, 1):
        where = [jax.random.randint(jax.random.fold_in(key, axis), (), 0, length) for axis, length in enumerate(array.shape)]
        where[longest] = (where[longest] + shift) % array.shape[longest]
        spots.append(tuple(where))
    return array.at[spots[0]].set(low).at[spots[1]].set(top_value)


def shard_levels(own_key, dims, cuts, low, high):
    def one(position, parts):
        draws = jax.random.uniform(jax.random.fold_in(jax.random.fold_in(own_key, 6), position), (parts,), jnp.float32, low / len(cuts), high / len(cuts))
        return jnp.repeat(jnp.exp(draws), dims[position] // parts).reshape((-1,) + (1,) * (len(dims) - position - 1))

    factor_of = one(*cuts[0])
    for cut in cuts[1:]:
        factor_of = factor_of * one(*cut)
    return factor_of


def setup_inputs(seed: int = 0) -> dict:
    streams_of = jax.random.split(jax.random.key(seed), 5)
    return {
        "field": jnp.clip(jnp.exp(math.log(2.0) - 2.9957323 * jax.random.uniform(streams_of[0], (NZ, NY, NX), jnp.float32) ** shard_levels(streams_of[0], (NZ, NY, NX), ((0, 4), (1, 4), (2, 2)), -0.2, 0.2)), 0.1, 2.0),
        "bins": set_ends(jax.random.randint(streams_of[1], (NZ, NY, NX), 0, NBINS), jax.random.fold_in(streams_of[1], 1), 0, NBINS - 1).astype(jnp.int32),
        "table": draw_table(jax.random.fold_in(streams_of[4], 71), 0),
        "march_order": set_ends(jax.random.randint(streams_of[3], (NY,), 0, 2), jax.random.fold_in(streams_of[3], 1), 0, 1).astype(jnp.int32),
    }


def reference(field, bins, table, march_order):
    padded = jnp.pad(field, 1)
    palette = table.astype(jnp.float32)
    depth = field.shape[0]

    def march(backward):

        def advance(carry, step):
            colour, trans = carry
            index = depth - 1 - step if backward else step
            index = jnp.asarray(index).astype(jnp.int32)
            window = lax.dynamic_slice_in_dim(padded, index, 3, 0)
            centre = window[1, 1:-1, 1:-1]
            grad_x = 0.5 * (window[1, 1:-1, 2:] - window[1, 1:-1, :-2])
            grad_y = 0.5 * (window[1, 2:, 1:-1] - window[1, :-2, 1:-1])
            grad_z = 0.5 * (window[2, 1:-1, 1:-1] - window[0, 1:-1, 1:-1])
            facing = 0.36 * grad_x + 0.48 * grad_y + 0.8 * grad_z
            length = jnp.sqrt(grad_x * grad_x + grad_y * grad_y + grad_z * grad_z + 1.0)
            shading = 0.3 + 0.7 * jnp.abs(facing) / length
            labels = lax.dynamic_index_in_dim(bins, index, 0, keepdims=False)
            looked = palette[:, labels]
            opacity = 1.0 - jnp.exp(-looked[3] * centre)
            emitted = looked[:3] * (shading * opacity)[None]
            colour = colour + trans[None] * emitted
            trans = trans * (1.0 - opacity)
            return ((colour, trans), None)
        start = (jnp.zeros((3,) + field.shape[1:], jnp.float32), jnp.ones(field.shape[1:], jnp.float32))
        (colour, trans), unused = lax.scan(advance, start, jnp.arange(depth, dtype=jnp.int32))
        return jnp.concatenate([colour, (1.0 - trans)[None]], 0)
    forward = march(False)
    backward = march(True)
    rowflip = (march_order == 1)[None, :, None]
    return jnp.where(rowflip, backward, forward)
```

```python
import functools

import jax
import jax.numpy as jnp
from jax import lax
from jax.experimental import pallas as pl
from jax.experimental.pallas import tpu as pltpu
from jax.sharding import PartitionSpec as P

light_x = 0.36
light_y = 0.48
light_z = 0.8
LANES = 128
ROWS = 8
WIDE = 512


def partner(x, axis, distance):
    return lax.ppermute(x, axis, [(i, i ^ distance) for i in range(lax.axis_size(axis))])


def shade_kernel(count, depth, place, *refs):
    bricks = refs[:count]
    edges = refs[count : 2 * count]
    beside = refs[2 * count]
    ordered, shading, ext = refs[2 * count + 1 :]
    rows, width = ordered.shape[1:]
    total = count * depth
    rank = place[0]
    side = place[1]
    zero_plane = jnp.zeros((rows, width), jnp.float32)
    ext[0, ROWS : ROWS + rows, LANES : LANES + width] = zero_plane
    ext[total + 1, ROWS : ROWS + rows, LANES : LANES + width] = zero_plane
    for slot in range(count):
        for j in range(depth):
            at = (rank ^ slot) * depth + j
            plane = bricks[slot][j]
            ordered[at] = plane
            ext[at + 1, ROWS : ROWS + rows, LANES : LANES + width] = plane
            ext[at + 1, ROWS - 1 : ROWS, LANES : LANES + width] = edges[slot][j : j + 1, :]
            ext[at + 1, ROWS + rows : ROWS + rows + 1, LANES : LANES + width] = edges[slot][depth + j : depth + j + 1, :]
            column = beside[slot * depth + j]
            ext[at + 1, ROWS : ROWS + rows, :LANES] = jnp.where(side == 1, column, 0.0)
            ext[at + 1, ROWS : ROWS + rows, LANES + width :] = jnp.where(side == 0, column, 0.0)

    def plane_step(at, _):
        for top in range(0, rows, ROWS):
            here = slice(ROWS + top, 2 * ROWS + top)
            for left in range(0, width, WIDE):
                cols = slice(LANES + left, LANES + left + WIDE)
                dx = (
                    ext[at + 1, here, LANES + left + 1 : LANES + left + 1 + WIDE]
                    - ext[at + 1, here, LANES + left - 1 : LANES + left - 1 + WIDE]
                )
                dy = (
                    ext[at + 1, ROWS + top + 1 : 2 * ROWS + top + 1, cols]
                    - ext[at + 1, ROWS + top - 1 : 2 * ROWS + top - 1, cols]
                )
                dz = ext[at + 2, here, cols] - ext[at, here, cols]
                facing = jnp.abs((0.5 * light_x) * dx + (0.5 * light_y) * dy + (0.5 * light_z) * dz)
                square = 0.25 * (dx * dx + dy * dy + dz * dz) + 1.0
                shading[at, top : top + ROWS, left : left + WIDE] = 0.3 + 0.7 * facing * lax.rsqrt(square)
        return 0

    lax.fori_loop(0, total, plane_step, 0)


def blend_kernel(count, depth, place, table, flips, ordered, shading, *refs):
    bricks = refs[:count]
    image = refs[-2]
    sorted_bins = refs[-1]
    total = count * depth
    rows, width = image.shape[1:]
    rank = place[0]
    for slot in range(count):
        for j in range(depth):
            sorted_bins[(rank ^ slot) * depth + j] = bricks[slot][j]
    palette = [table[c] for c in range(4)]
    back = flips[...] == 1

    def look(entries, labels):
        return jnp.take_along_axis(entries, labels, axis=1, mode="promise_in_bounds")

    def tile_step(step, _):
        cols = pl.ds(pl.multiple_of(step * LANES, LANES), LANES)
        labels = [sorted_bins[d, :, cols] for d in range(total)]
        sums = [jnp.zeros((rows, LANES), jnp.float32)]
        for d in range(total):
            sums.append(sums[-1] + look(palette[3], labels[d]) * ordered[d, :, cols])
        whole = sums[-1]
        through = [jnp.exp(-jnp.where(back, whole - s, s)) for s in sums]
        colour = [jnp.zeros((rows, LANES), jnp.float32) for _ in range(3)]
        for d in range(total):
            weight = jnp.abs(through[d] - through[d + 1]) * shading[d, :, cols]
            for c in range(3):
                colour[c] = colour[c] + weight * look(palette[c], labels[d])
        for c in range(3):
            image[c, :, cols] = colour[c]
        image[3, :, cols] = 1.0 - jnp.exp(-whole)
        return 0

    lax.fori_loop(0, width // LANES, tile_step, 0)


def shards(field, bins, table, march_order):
    depth, height, width = field.shape
    count = lax.axis_size("gz")
    rank = lax.axis_index("gz").astype(jnp.int32)
    side = lax.axis_index("sx").astype(jnp.int32)
    place = jnp.stack([rank, side])
    rows = height // count
    total = count * depth
    cuts = [(0, rows)] if rows <= ROWS else [(0, rows - ROWS), (rows - ROWS, ROWS)]

    def piece(array, slot, start, size):
        return lax.dynamic_slice_in_dim(array, (rank ^ slot) * rows + start, size, axis=1)

    def scatter(pieces):
        return [pieces[0]] + [partner(pieces[slot], "gz", slot) for slot in range(1, count)]

    slots = range(count)
    field_bricks = scatter([piece(field, slot, 0, rows) for slot in slots])

    forward = [(i, i + 1) for i in range(lax.axis_size("sy") - 1)]
    backward = [(target, source) for source, target in forward]
    above = lax.ppermute(field[:, height - 1 :], "sy", forward)
    below = lax.ppermute(field[:, :1], "sy", backward)
    tops = jnp.concatenate([above, field[:, rows - 1 : height - 1 : rows]], axis=1)
    bottoms = jnp.concatenate([field[:, rows::rows], below], axis=1)
    edge_rows = jnp.concatenate([tops, bottoms], axis=0)
    edges = scatter(
        [lax.dynamic_index_in_dim(edge_rows, rank ^ slot, axis=1, keepdims=False) for slot in slots]
    )

    bins_bricks = [
        scatter([piece(bins, slot, start, size) for slot in slots]) for start, size in cuts
    ]

    edge_column = (1 - side) * (width - LANES)
    slab = jnp.concatenate(
        [lax.dynamic_slice_in_dim(brick, edge_column, LANES, axis=2) for brick in field_bricks], axis=0
    )
    beside = partner(slab, "sx", 1)

    vmem = pl.BlockSpec(memory_space=pltpu.VMEM)
    smem = pl.BlockSpec(memory_space=pltpu.SMEM)
    planes = jax.ShapeDtypeStruct((total, rows, width), jnp.float32)
    ordered, shading = pl.pallas_call(
        functools.partial(shade_kernel, count, depth),
        out_shape=(planes, planes),
        in_specs=[smem] + [vmem] * (2 * count + 1),
        out_specs=(vmem, vmem),
        scratch_shapes=[pltpu.VMEM((total + 2, rows + 2 * ROWS, width + 2 * LANES), jnp.float32)],
        compiler_params=pltpu.CompilerParams(vmem_limit_bytes=40 * 1024 * 1024),
        cost_estimate=pl.CostEstimate(
            flops=20 * total * rows * width, bytes_accessed=16 * total * rows * width, transcendentals=total * rows * width
        ),
        name="shade",
    )(place, *field_bricks, *edges, beside)

    flips = lax.dynamic_slice_in_dim(march_order, rank * rows, rows, axis=0)
    flips = jnp.broadcast_to(flips[:, None], (rows, LANES))
    palette = jnp.broadcast_to(table.astype(jnp.float32)[:, None, :], (4, ROWS, table.shape[1]))

    image = None
    for (start, size), bricks in zip(cuts, bins_bricks):
        first = start // ROWS
        plane_spec = pl.BlockSpec((total, ROWS, width), lambda i, first=first: (0, first + i, 0))
        in_specs = [
            smem,
            pl.BlockSpec((4, ROWS, table.shape[1]), lambda i: (0, 0, 0)),
            pl.BlockSpec((ROWS, LANES), lambda i, first=first: (first + i, 0)),
            plane_spec,
            plane_spec,
        ] + [pl.BlockSpec((depth, ROWS, width), lambda i: (0, i, 0))] * count
        operands = [place, palette, flips, ordered, shading, *bricks]
        aliases = {}
        if image is not None:
            in_specs.append(pl.BlockSpec(memory_space=pl.ANY))
            aliases = {len(operands): 0}
            operands.append(image)
        image = pl.pallas_call(
            functools.partial(blend_kernel, count, depth),
            grid=(size // ROWS,),
            out_shape=jax.ShapeDtypeStruct((4, rows, width), jnp.float32),
            in_specs=in_specs,
            out_specs=pl.BlockSpec((4, ROWS, width), lambda i, first=first: (0, first + i, 0)),
            scratch_shapes=[pltpu.VMEM((total, ROWS, width), jnp.int32)],
            input_output_aliases=aliases,
            compiler_params=pltpu.CompilerParams(vmem_limit_bytes=40 * 1024 * 1024),
            cost_estimate=pl.CostEstimate(
                flops=20 * total * size * width, bytes_accessed=16 * total * size * width, transcendentals=total * size * width
            ),
            name="blend",
        )(*operands)
    return image


def solution(mesh):
    placed = (P("gz", "sy", "sx"), P("gz", "sy", "sx"), P(), P("sy"))
    return jax.shard_map(
        shards, mesh=mesh, in_specs=placed, out_specs=P(None, ("sy", "gz"), "sx"), check_vma=False
    )
```

```python
import functools

import jax
import jax.numpy as jnp
from jax import lax
from jax.experimental import pallas as pl
from jax.experimental.pallas import tpu as pltpu
from jax.sharding import PartitionSpec as P

light_x = 0.36
light_y = 0.48
light_z = 0.8
LANES = 128
ROWS = 8
GROUP = 4
COLOUR_UNIT = 2.0**-12
OPACITY_UNIT = 2.0**-13
HALF_WORD = 16
VMEM_LIMIT = 40 * 1024 * 1024

vmem = pl.BlockSpec(memory_space=pltpu.VMEM)
smem = pl.BlockSpec(memory_space=pltpu.SMEM)
anywhere = pl.BlockSpec(memory_space=pl.ANY)


def partner(x, axis, distance):
    return lax.ppermute(x, axis, [(i, i ^ distance) for i in range(lax.axis_size(axis))])


def pack_kernel(count, depth, place, above, below, field, bins, *refs):
    messages = refs[:count]
    high, low, labels, sems = refs[count:]
    height, width = field.shape[1:]
    rows = height // count
    half = width // 2
    rank = place[0]
    copies = []
    for slot in range(count):
        target = rank ^ slot
        top = pl.multiple_of(jnp.maximum(target * rows - ROWS, 0), ROWS)
        bottom = pl.multiple_of(jnp.minimum(target * rows + rows, height - ROWS), ROWS)
        start = pl.multiple_of(target * rows, ROWS)
        moves = [
            pltpu.make_async_copy(field.at[:, pl.ds(top, ROWS)], high.at[slot], sems.at[slot, 0]),
            pltpu.make_async_copy(field.at[:, pl.ds(bottom, ROWS)], low.at[slot], sems.at[slot, 1]),
        ]
        if slot:
            moves.append(pltpu.make_async_copy(bins.at[:, pl.ds(start, ROWS)], labels.at[slot], sems.at[slot, 2]))
        for move in moves:
            move.start()
        copies.append(moves)
    for slot in range(count):
        target = rank ^ slot
        for move in copies[slot]:
            move.wait()
        for j in range(depth):
            upper = jnp.where(target == 0, above[j : j + 1, :], high[slot, j, ROWS - 1 : ROWS, :])
            lower = jnp.where(target == count - 1, below[j : j + 1, :], low[slot, j, 0:1, :])
            for h in range(2):
                cols = slice(h * half, (h + 1) * half)
                at = 2 * depth * h + j
                messages[slot][at : at + 1, :] = upper[:, cols]
                messages[slot][at + depth : at + depth + 1, :] = lower[:, cols]
                if slot:
                    first = 4 * depth + (2 * j + h) * ROWS
                    messages[slot][first : first + ROWS, :] = labels[slot, j, :, cols].astype(jnp.float32)


def shade_kernel(count, depth, place, *refs):
    bricks = refs[:count]
    messages = refs[count : 2 * count]
    beside = refs[2 * count]
    ordered, shading, ext = refs[2 * count + 1 :]
    rows, width = ordered.shape[1:]
    half = width // 2
    total = count * depth
    rank = place[0]
    side = place[1]
    inside = slice(ROWS, ROWS + rows)
    zero_plane = jnp.zeros((rows, width), jnp.float32)
    ext[0, inside, LANES : LANES + width] = zero_plane
    ext[total + 1, inside, LANES : LANES + width] = zero_plane
    for slot in range(count):
        for j in range(depth):
            at = (rank ^ slot) * depth + j
            plane = bricks[slot][j]
            ordered[at] = plane * OPACITY_UNIT
            ext[at + 1, inside, LANES : LANES + width] = plane
            for h in range(2):
                cols = slice(LANES + h * half, LANES + (h + 1) * half)
                row = 2 * depth * h + j
                ext[at + 1, ROWS - 1 : ROWS, cols] = messages[slot][row : row + 1, :]
                ext[at + 1, ROWS + rows : ROWS + rows + 1, cols] = messages[slot][row + depth : row + depth + 1, :]
            column = beside[slot * depth + j]
            ext[at + 1, inside, :LANES] = jnp.where(side == 1, column, 0.0)
            ext[at + 1, inside, LANES + width :] = jnp.where(side == 0, column, 0.0)
    lane = lax.broadcasted_iota(jnp.int32, (ROWS, LANES), 1)
    first = lane == 0
    last = lane == LANES - 1

    def plane_step(at, _):
        for top in range(0, rows, ROWS):
            here = slice(ROWS + top, 2 * ROWS + top)
            tiles = [ext[at + 1, here, left : left + LANES] for left in range(0, width + 2 * LANES, LANES)]
            toward = [pltpu.roll(tile, LANES - 1, 1) for tile in tiles]
            away = [pltpu.roll(tile, 1, 1) for tile in tiles]
            for c in range(1, width // LANES + 1):
                cols = slice(c * LANES, (c + 1) * LANES)
                dx = jnp.where(last, toward[c + 1], toward[c]) - jnp.where(first, away[c - 1], away[c])
                dy = (
                    ext[at + 1, ROWS + top + 1 : 2 * ROWS + top + 1, cols]
                    - ext[at + 1, ROWS + top - 1 : 2 * ROWS + top - 1, cols]
                )
                dz = ext[at + 2, here, cols] - ext[at, here, cols]
                facing = jnp.abs((0.5 * light_x) * dx + (0.5 * light_y) * dy + (0.5 * light_z) * dz)
                square = 0.25 * (dx * dx + dy * dy + dz * dz) + 1.0
                shading[at, top : top + ROWS, (c - 1) * LANES : c * LANES] = (
                    0.3 * COLOUR_UNIT + (0.7 * COLOUR_UNIT) * facing * lax.rsqrt(square)
                )
        return 0

    lax.fori_loop(0, total, plane_step, 0)


def blend_kernel(count, depth, start, packed, place, table, flips, ordered, shading, *refs):
    bricks = refs[:count]
    image, sorted_bins, result, sems = refs[-4:]
    total = count * depth
    rows, width = result.shape[1:]
    half = width // 2
    rank = place[0]
    for slot in range(count):
        for j in range(depth):
            at = (rank ^ slot) * depth + j
            if packed and slot:
                for h in range(2):
                    top = 4 * depth + (2 * j + h) * ROWS
                    values = bricks[slot][top : top + ROWS, :]
                    sorted_bins[at, :, h * half : (h + 1) * half] = values.astype(jnp.int32)
            else:
                sorted_bins[at] = bricks[slot][j]
    entries = [table[c] for c in range(2)]
    wide = GROUP * LANES
    groups = width // wide

    def copy(top, step):
        cols = pl.ds(pl.multiple_of(step * wide, wide), wide)
        return pltpu.make_async_copy(
            result.at[:, top : top + ROWS, cols],
            image.at[:, start + top : start + top + ROWS, cols],
            sems.at[top // ROWS, step],
        )

    def look(values, labels):
        return jnp.take_along_axis(values, labels, axis=1, mode="promise_in_bounds")

    def low_part(words):
        return (words & ((1 << HALF_WORD) - 1)).astype(jnp.float32)

    def high_part(words):
        return (words >> HALF_WORD).astype(jnp.float32)

    for top in range(0, rows, ROWS):
        here = slice(top, top + ROWS)
        span = slice(start + top, start + top + ROWS)
        back = flips[span, :] == 1

        def group_step(step, _):
            for tile in range(GROUP):
                cols = pl.ds(pl.multiple_of((step * GROUP + tile) * LANES, LANES), LANES)
                labels = [sorted_bins[d, here, cols] for d in range(total)]
                second = [look(entries[1], labels[d]) for d in range(total)]
                sums = [jnp.zeros((ROWS, LANES), jnp.float32)]
                for d in range(total):
                    sums.append(sums[-1] + high_part(second[d]) * ordered[d, span, cols])
                whole = sums[-1]
                through = [jnp.exp(-jnp.where(back, whole - s, s)) for s in sums]
                colour = [jnp.zeros((ROWS, LANES), jnp.float32) for _ in range(3)]
                for d in range(total):
                    weight = jnp.abs(through[d] - through[d + 1]) * shading[d, span, cols]
                    first = look(entries[0], labels[d])
                    colour[0] = colour[0] + weight * low_part(first)
                    colour[1] = colour[1] + weight * high_part(first)
                    colour[2] = colour[2] + weight * low_part(second[d])
                for c in range(3):
                    result[c, here, cols] = colour[c]
                result[3, here, cols] = 1.0 - jnp.exp(-whole)
            copy(top, step).start()
            return 0

        lax.fori_loop(0, groups, group_step, 0)

    for top in range(0, rows, ROWS):
        for step in range(groups):
            copy(top, step).wait()


def shards(field, bins, table, march_order):
    depth, height, width = field.shape
    count = lax.axis_size("gz")
    rank = lax.axis_index("gz").astype(jnp.int32)
    side = lax.axis_index("sx").astype(jnp.int32)
    place = jnp.stack([rank, side])
    rows = height // count
    total = count * depth
    cuts = [(0, ROWS)]
    if rows > 2 * ROWS:
        cuts.append((ROWS, rows - 2 * ROWS))
    if rows > ROWS:
        cuts.append((rows - ROWS, ROWS))
    partners = sorted(range(1, count), key=lambda slot: (-slot.bit_count(), slot))

    def piece(array, slot, start, size):
        return lax.dynamic_slice_in_dim(array, (rank ^ slot) * rows + start, size, axis=1)

    def after(array, *others):
        return lax.optimization_barrier((array, *others))[0]

    own_field = piece(field, 0, 0, rows)
    field_bricks = {0: own_field}
    source = field
    for slot in partners:
        cut = piece(source, slot, 0, rows)
        source = after(field, cut)
        field_bricks[slot] = partner(cut, "gz", slot)

    forward = [(i, i + 1) for i in range(lax.axis_size("sy") - 1)]
    backward = [(target, origin) for origin, target in forward]
    above = lax.ppermute(source[:, height - 1], "sy", forward)
    below = lax.ppermute(source[:, 0], "sy", backward)

    half = width // 2
    edge_rows = 4 * depth
    message_rows = edge_rows + 2 * depth * ROWS
    messages = pl.pallas_call(
        functools.partial(pack_kernel, count, depth),
        out_shape=[
            jax.ShapeDtypeStruct((message_rows if slot else edge_rows, half), jnp.float32) for slot in range(count)
        ],
        in_specs=[smem, vmem, vmem, anywhere, anywhere],
        out_specs=[vmem] * count,
        scratch_shapes=[
            pltpu.VMEM((count, depth, ROWS, width), jnp.float32),
            pltpu.VMEM((count, depth, ROWS, width), jnp.float32),
            pltpu.VMEM((count, depth, ROWS, width), jnp.int32),
            pltpu.SemaphoreType.DMA((count, 3)),
        ],
        compiler_params=pltpu.CompilerParams(vmem_limit_bytes=VMEM_LIMIT),
        cost_estimate=pl.CostEstimate(flops=0, bytes_accessed=8 * count * message_rows * half, transcendentals=0),
        name="pack",
    )(place, above, below, field, bins)
    later_bins = after(bins, *messages)
    arrived = {0: messages[0]}
    for slot in partners:
        arrived[slot] = partner(messages[slot], "gz", slot)

    bins_bricks = [[piece(bins, 0, *cuts[0])] + [arrived[slot] for slot in range(1, count)]]
    for start, size in cuts[1:]:
        own = piece(bins, 0, start, size)
        bricks = {0: own}
        cut = [piece(later_bins, slot, start, size) for slot in partners]
        later_bins = after(bins, *cut)
        for slot, sent in zip(partners, cut):
            bricks[slot] = partner(sent, "gz", slot)
        bins_bricks.append([bricks[slot] for slot in range(count)])

    edge_column = (1 - side) * (width - LANES)
    slab = jnp.concatenate(
        [lax.dynamic_slice_in_dim(field_bricks[slot], edge_column, LANES, axis=2) for slot in range(count)], axis=0
    )
    beside = partner(slab, "sx", 1)

    cells = total * rows * width
    planes = jax.ShapeDtypeStruct((total, rows, width), jnp.float32)
    ordered, shading = pl.pallas_call(
        functools.partial(shade_kernel, count, depth),
        out_shape=(planes, planes),
        in_specs=[smem] + [vmem] * (2 * count + 1),
        out_specs=(vmem, vmem),
        scratch_shapes=[pltpu.VMEM((total + 2, rows + 2 * ROWS, width + 2 * LANES), jnp.float32)],
        compiler_params=pltpu.CompilerParams(vmem_limit_bytes=VMEM_LIMIT),
        cost_estimate=pl.CostEstimate(flops=20 * cells, bytes_accessed=16 * cells, transcendentals=cells),
        name="shade",
    )(place, *[field_bricks[slot] for slot in range(count)], *[arrived[slot] for slot in range(count)], beside)

    flips = lax.dynamic_slice_in_dim(march_order, rank * rows, rows, axis=0)
    flips = jnp.broadcast_to(flips[:, None], (rows, LANES))
    colours = (table[:3].astype(jnp.float32) * (1.0 / COLOUR_UNIT)).astype(jnp.int32)
    opacity = (table[3].astype(jnp.float32) * (1.0 / OPACITY_UNIT)).astype(jnp.int32)
    entries = jnp.stack([colours[0] | colours[1] << HALF_WORD, colours[2] | opacity << HALF_WORD])
    entries = jnp.broadcast_to(entries[:, None, :], (2, ROWS, table.shape[1]))

    image = None
    for index, ((start, size), bricks) in enumerate(zip(cuts, bins_bricks)):
        operands = [place, entries, flips, ordered, shading, *bricks]
        in_specs = [smem] + [vmem] * (len(operands) - 1)
        aliases = {}
        if image is not None:
            in_specs.append(anywhere)
            aliases = {len(operands): 0}
            operands.append(image)
        cells = total * size * width
        image = pl.pallas_call(
            functools.partial(blend_kernel, count, depth, start, index == 0),
            out_shape=jax.ShapeDtypeStruct((4, rows, width), jnp.float32),
            in_specs=in_specs,
            out_specs=anywhere,
            scratch_shapes=[
                pltpu.VMEM((total, size, width), jnp.int32),
                pltpu.VMEM((4, size, width), jnp.float32),
                pltpu.SemaphoreType.DMA((size // ROWS, width // (GROUP * LANES))),
            ],
            input_output_aliases=aliases,
            compiler_params=pltpu.CompilerParams(vmem_limit_bytes=VMEM_LIMIT),
            cost_estimate=pl.CostEstimate(flops=20 * cells, bytes_accessed=16 * cells, transcendentals=cells),
            name="blend",
        )(*operands)
    return image


def solution(mesh):
    placed = (P("gz", "sy", "sx"), P("gz", "sy", "sx"), P(), P("sy"))
    return jax.shard_map(
        shards, mesh=mesh, in_specs=placed, out_specs=P(None, ("sy", "gz"), "sx"), check_vma=False
    )
```

```python
import functools

import jax
import jax.numpy as jnp
from jax import lax
from jax.experimental import pallas as pl
from jax.experimental.pallas import tpu as pltpu
from jax.sharding import PartitionSpec as P

light_x = 0.36
light_y = 0.48
light_z = 0.8
LANES = 128
ROWS = 8
GROUP = 4
COLOUR_UNIT = 2.0**-12
OPACITY_UNIT = 2.0**-13
HALF_WORD = 16
VMEM_LIMIT = 40 * 1024 * 1024

vmem = pl.BlockSpec(memory_space=pltpu.VMEM)
hbm = pl.BlockSpec(memory_space=pltpu.HBM)


def partner(x, axis, distance):
    return lax.ppermute(x, axis, [(i, i ^ distance) for i in range(lax.axis_size(axis))])


def split_kernel(count, depth, slots, field, *refs):
    pieces = refs[: len(slots)]
    last, first, ends, sems = refs[len(slots) :]
    height = field.shape[1]
    rows = height // count
    rank = lax.axis_index("gz")
    moves = [
        pltpu.make_async_copy(field.at[:, height - ROWS :], ends.at[0], sems.at[0]),
        pltpu.make_async_copy(field.at[:, :ROWS], ends.at[1], sems.at[1]),
    ]
    for index, slot in enumerate(slots):
        start = pl.multiple_of((rank ^ slot) * rows, ROWS)
        moves.append(pltpu.make_async_copy(field.at[:, pl.ds(start, rows)], pieces[index], sems.at[2 + index]))
    for move in moves:
        move.start()
    for move in moves:
        move.wait()
    for j in range(depth):
        last[j : j + 1, :] = ends[0, j, ROWS - 1 :, :]
        first[j : j + 1, :] = ends[1, j, :1, :]


def pack_kernel(count, depth, above, below, field, bins, *refs):
    messages = refs[:count]
    high, low, labels, sems = refs[count:]
    height, width = field.shape[1:]
    rows = height // count
    half = width // 2
    rank = lax.axis_index("gz")
    copies = []
    for slot in range(count):
        target = rank ^ slot
        top = pl.multiple_of(jnp.maximum(target * rows - ROWS, 0), ROWS)
        bottom = pl.multiple_of(jnp.minimum(target * rows + rows, height - ROWS), ROWS)
        start = pl.multiple_of(target * rows, ROWS)
        moves = [
            pltpu.make_async_copy(field.at[:, pl.ds(top, ROWS)], high.at[slot], sems.at[slot, 0]),
            pltpu.make_async_copy(field.at[:, pl.ds(bottom, ROWS)], low.at[slot], sems.at[slot, 1]),
        ]
        if slot:
            moves.append(pltpu.make_async_copy(bins.at[:, pl.ds(start, ROWS)], labels.at[slot], sems.at[slot, 2]))
        for move in moves:
            move.start()
        copies.append(moves)
    for slot in range(count):
        target = rank ^ slot
        for move in copies[slot]:
            move.wait()
        for j in range(depth):
            upper = jnp.where(target == 0, above[j : j + 1, :], high[slot, j, ROWS - 1 : ROWS, :])
            lower = jnp.where(target == count - 1, below[j : j + 1, :], low[slot, j, 0:1, :])
            for h in range(2):
                cols = slice(h * half, (h + 1) * half)
                at = 2 * depth * h + j
                messages[slot][at : at + 1, :] = upper[:, cols]
                messages[slot][at + depth : at + depth + 1, :] = lower[:, cols]
                if slot:
                    first = 4 * depth + (2 * j + h) * ROWS
                    messages[slot][first : first + ROWS, :] = labels[slot, j, :, cols].astype(jnp.float32)


def shade_kernel(count, depth, *refs):
    bricks = refs[:count]
    messages = refs[count : 2 * count]
    beside = refs[2 * count]
    ordered, shading, ext = refs[2 * count + 1 :]
    rows, width = ordered.shape[1:]
    half = width // 2
    total = count * depth
    rank = lax.axis_index("gz")
    side = lax.axis_index("sx")
    inside = slice(ROWS, ROWS + rows)
    zero_plane = jnp.zeros((rows, width), jnp.float32)
    ext[0, inside, LANES : LANES + width] = zero_plane
    ext[total + 1, inside, LANES : LANES + width] = zero_plane
    for slot in range(count):
        for j in range(depth):
            at = (rank ^ slot) * depth + j
            plane = bricks[slot][j]
            ordered[at] = plane * OPACITY_UNIT
            ext[at + 1, inside, LANES : LANES + width] = plane
            for h in range(2):
                cols = slice(LANES + h * half, LANES + (h + 1) * half)
                row = 2 * depth * h + j
                ext[at + 1, ROWS - 1 : ROWS, cols] = messages[slot][row : row + 1, :]
                ext[at + 1, ROWS + rows : ROWS + rows + 1, cols] = messages[slot][row + depth : row + depth + 1, :]
            column = beside[slot * depth + j]
            ext[at + 1, inside, :LANES] = jnp.where(side == 1, column, 0.0)
            ext[at + 1, inside, LANES + width :] = jnp.where(side == 0, column, 0.0)
    lane = lax.broadcasted_iota(jnp.int32, (ROWS, LANES), 1)
    first = lane == 0
    last = lane == LANES - 1

    def plane_step(at, _):
        for top in range(0, rows, ROWS):
            here = slice(ROWS + top, 2 * ROWS + top)
            tiles = [ext[at + 1, here, left : left + LANES] for left in range(0, width + 2 * LANES, LANES)]
            toward = [pltpu.roll(tile, LANES - 1, 1) for tile in tiles]
            away = [pltpu.roll(tile, 1, 1) for tile in tiles]
            for c in range(1, width // LANES + 1):
                cols = slice(c * LANES, (c + 1) * LANES)
                dx = jnp.where(last, toward[c + 1], toward[c]) - jnp.where(first, away[c - 1], away[c])
                dy = (
                    ext[at + 1, ROWS + top + 1 : 2 * ROWS + top + 1, cols]
                    - ext[at + 1, ROWS + top - 1 : 2 * ROWS + top - 1, cols]
                )
                dz = ext[at + 2, here, cols] - ext[at, here, cols]
                facing = jnp.abs((0.5 * light_x) * dx + (0.5 * light_y) * dy + (0.5 * light_z) * dz)
                square = 0.25 * (dx * dx + dy * dy + dz * dz) + 1.0
                shading[at, top : top + ROWS, (c - 1) * LANES : c * LANES] = (
                    0.3 * COLOUR_UNIT + (0.7 * COLOUR_UNIT) * facing * lax.rsqrt(square)
                )
        return 0

    lax.fori_loop(0, total, plane_step, 0)


def blend_kernel(count, depth, start, packed, table, flips, ordered, shading, *refs):
    bricks = refs[:count]
    image, sorted_bins, result, sems = refs[-4:]
    total = count * depth
    rows, width = result.shape[1:]
    half = width // 2
    rank = lax.axis_index("gz")
    for slot in range(count):
        for j in range(depth):
            at = (rank ^ slot) * depth + j
            if packed and slot:
                for h in range(2):
                    top = 4 * depth + (2 * j + h) * ROWS
                    values = bricks[slot][top : top + ROWS, :]
                    sorted_bins[at, :, h * half : (h + 1) * half] = values.astype(jnp.int32)
            else:
                sorted_bins[at] = bricks[slot][j]
    entries = [table[c] for c in range(2)]
    wide = GROUP * LANES
    groups = width // wide

    def copy(top, step):
        cols = pl.ds(pl.multiple_of(step * wide, wide), wide)
        return pltpu.make_async_copy(
            result.at[:, top : top + ROWS, cols],
            image.at[:, start + top : start + top + ROWS, cols],
            sems.at[top // ROWS, step],
        )

    def look(values, labels):
        return jnp.take_along_axis(values, labels, axis=1, mode="promise_in_bounds")

    def low_part(words):
        return (words & ((1 << HALF_WORD) - 1)).astype(jnp.float32)

    def high_part(words):
        return (words >> HALF_WORD).astype(jnp.float32)

    for top in range(0, rows, ROWS):
        here = slice(top, top + ROWS)
        span = slice(start + top, start + top + ROWS)
        back = flips[span, :] == 1

        def group_step(step, _):
            for tile in range(GROUP):
                cols = pl.ds(pl.multiple_of((step * GROUP + tile) * LANES, LANES), LANES)
                labels = [sorted_bins[d, here, cols] for d in range(total)]
                second = [look(entries[1], labels[d]) for d in range(total)]
                sums = [jnp.zeros((ROWS, LANES), jnp.float32)]
                for d in range(total):
                    sums.append(sums[-1] + high_part(second[d]) * ordered[d, span, cols])
                whole = sums[-1]
                through = [jnp.exp(-jnp.where(back, whole - s, s)) for s in sums]
                colour = [jnp.zeros((ROWS, LANES), jnp.float32) for _ in range(3)]
                for d in range(total):
                    weight = jnp.abs(through[d] - through[d + 1]) * shading[d, span, cols]
                    first = look(entries[0], labels[d])
                    colour[0] = colour[0] + weight * low_part(first)
                    colour[1] = colour[1] + weight * high_part(first)
                    colour[2] = colour[2] + weight * low_part(second[d])
                for c in range(3):
                    result[c, here, cols] = colour[c]
                result[3, here, cols] = 1.0 - jnp.exp(-whole)
            copy(top, step).start()
            return 0

        lax.fori_loop(0, groups, group_step, 0)

    for top in range(0, rows, ROWS):
        for step in range(groups):
            copy(top, step).wait()


def shards(field, bins, table, march_order):
    depth, height, width = field.shape
    count = lax.axis_size("gz")
    rank = lax.axis_index("gz").astype(jnp.int32)
    side = lax.axis_index("sx").astype(jnp.int32)
    rows = height // count
    total = count * depth
    cuts = [(0, ROWS)]
    if rows > 2 * ROWS:
        cuts.append((ROWS, rows - 2 * ROWS))
    if rows > ROWS:
        cuts.append((rows - ROWS, ROWS))
    partners = sorted(range(1, count), key=lambda slot: (-slot.bit_count(), slot))

    def piece(array, slot, start, size):
        return lax.dynamic_slice_in_dim(array, (rank ^ slot) * rows + start, size, axis=1)

    def after(array, *others):
        return lax.optimization_barrier((array, *others))[0]

    lead = piece(field, partners[0], 0, rows)
    field_bricks = {partners[0]: partner(lead, "gz", partners[0])}
    *cut, last, first = pl.pallas_call(
        functools.partial(split_kernel, count, depth, partners[1:]),
        out_shape=[jax.ShapeDtypeStruct((depth, rows, width), jnp.float32)] * (count - 2)
        + [jax.ShapeDtypeStruct((depth, width), jnp.float32)] * 2,
        in_specs=[hbm],
        out_specs=[vmem] * count,
        scratch_shapes=[pltpu.VMEM((2, depth, ROWS, width), jnp.float32), pltpu.SemaphoreType.DMA((count,))],
        compiler_params=pltpu.CompilerParams(vmem_limit_bytes=VMEM_LIMIT),
        cost_estimate=pl.CostEstimate(flops=0, bytes_accessed=8 * count * depth * rows * width, transcendentals=0),
        name="split",
    )(after(field, lead))
    for slot, sent in zip(partners[1:], cut):
        field_bricks[slot] = partner(sent, "gz", slot)
    field_bricks[0] = piece(after(field, *cut), 0, 0, rows)

    forward = [(i, i + 1) for i in range(lax.axis_size("sy") - 1)]
    backward = [(target, origin) for origin, target in forward]
    above = lax.ppermute(last, "sy", forward)
    below = lax.ppermute(first, "sy", backward)

    half = width // 2
    edge_rows = 4 * depth
    message_rows = edge_rows + 2 * depth * ROWS
    messages = pl.pallas_call(
        functools.partial(pack_kernel, count, depth),
        out_shape=[
            jax.ShapeDtypeStruct((message_rows if slot else edge_rows, half), jnp.float32) for slot in range(count)
        ],
        in_specs=[vmem, vmem, hbm, hbm],
        out_specs=[vmem] * count,
        scratch_shapes=[
            pltpu.VMEM((count, depth, ROWS, width), jnp.float32),
            pltpu.VMEM((count, depth, ROWS, width), jnp.float32),
            pltpu.VMEM((count, depth, ROWS, width), jnp.int32),
            pltpu.SemaphoreType.DMA((count, 3)),
        ],
        compiler_params=pltpu.CompilerParams(vmem_limit_bytes=VMEM_LIMIT),
        cost_estimate=pl.CostEstimate(flops=0, bytes_accessed=8 * count * message_rows * half, transcendentals=0),
        name="pack",
    )(above, below, field, bins)
    later_bins = after(bins, *messages)
    arrived = {0: messages[0]}
    for slot in partners:
        arrived[slot] = partner(messages[slot], "gz", slot)

    edge_column = (1 - side) * (width - LANES)
    slab = jnp.concatenate(
        [lax.dynamic_slice_in_dim(field_bricks[slot], edge_column, LANES, axis=2) for slot in range(count)], axis=0
    )
    beside = partner(slab, "sx", 1)

    cells = total * rows * width
    planes = jax.ShapeDtypeStruct((total, rows, width), jnp.float32)
    ordered, shading = pl.pallas_call(
        functools.partial(shade_kernel, count, depth),
        out_shape=(planes, planes),
        in_specs=[vmem] * (2 * count + 1),
        out_specs=(vmem, vmem),
        scratch_shapes=[pltpu.VMEM((total + 2, rows + 2 * ROWS, width + 2 * LANES), jnp.float32)],
        compiler_params=pltpu.CompilerParams(vmem_limit_bytes=VMEM_LIMIT),
        cost_estimate=pl.CostEstimate(flops=20 * cells, bytes_accessed=16 * cells, transcendentals=cells),
        name="shade",
    )(*[field_bricks[slot] for slot in range(count)], *[arrived[slot] for slot in range(count)], beside)

    bins_bricks = [[piece(bins, 0, *cuts[0])] + [arrived[slot] for slot in range(1, count)]]
    for index, (start, size) in enumerate(cuts[1:]):
        if index:
            later_bins = after(later_bins, shading)
        own = piece(bins, 0, start, size)
        bricks = {0: own}
        cut = [piece(later_bins, slot, start, size) for slot in partners]
        later_bins = after(bins, *cut)
        for slot, sent in zip(partners, cut):
            bricks[slot] = partner(sent, "gz", slot)
        bins_bricks.append([bricks[slot] for slot in range(count)])

    flips = lax.dynamic_slice_in_dim(march_order, rank * rows, rows, axis=0)
    flips = jnp.broadcast_to(flips[:, None], (rows, LANES))
    colours = (table[:3].astype(jnp.float32) * (1.0 / COLOUR_UNIT)).astype(jnp.int32)
    opacity = (table[3].astype(jnp.float32) * (1.0 / OPACITY_UNIT)).astype(jnp.int32)
    entries = jnp.stack([colours[0] | colours[1] << HALF_WORD, colours[2] | opacity << HALF_WORD])
    entries = jnp.broadcast_to(entries[:, None, :], (2, ROWS, table.shape[1]))

    image = None
    for index, ((start, size), bricks) in enumerate(zip(cuts, bins_bricks)):
        operands = [entries, flips, ordered, shading, *bricks]
        in_specs = [vmem] * len(operands)
        aliases = {}
        if image is not None:
            in_specs.append(hbm)
            aliases = {len(operands): 0}
            operands.append(image)
        cells = total * size * width
        image = pl.pallas_call(
            functools.partial(blend_kernel, count, depth, start, index == 0),
            out_shape=jax.ShapeDtypeStruct((4, rows, width), jnp.float32),
            in_specs=in_specs,
            out_specs=hbm,
            scratch_shapes=[
                pltpu.VMEM((total, size, width), jnp.int32),
                pltpu.VMEM((4, size, width), jnp.float32),
                pltpu.SemaphoreType.DMA((size // ROWS, width // (GROUP * LANES))),
            ],
            input_output_aliases=aliases,
            compiler_params=pltpu.CompilerParams(vmem_limit_bytes=VMEM_LIMIT),
            cost_estimate=pl.CostEstimate(flops=20 * cells, bytes_accessed=16 * cells, transcendentals=cells),
            name="blend",
        )(*operands)
    return image


def solution(mesh):
    placed = (P("gz", "sy", "sx"), P("gz", "sy", "sx"), P(), P("sy"))
    return jax.shard_map(
        shards, mesh=mesh, in_specs=placed, out_specs=P(None, ("sy", "gz"), "sx"), check_vma=False
    )
```

```python
import functools

import jax
import jax.numpy as jnp
from jax import lax
from jax.experimental import pallas as pl
from jax.experimental.pallas import tpu as pltpu
from jax.sharding import PartitionSpec as P

light_x = 0.36
light_y = 0.48
light_z = 0.8
LANES = 128
ROWS = 8
COLOUR_UNIT = 2.0**-12
OPACITY_UNIT = 2.0**-13
HALF_WORD = 16
LOG2_E = 1.4426950408889634
UNROLLED = 32
COPIES = 4
VMEM_LIMIT = 40 * 1024 * 1024

vmem = pl.BlockSpec(memory_space=pltpu.VMEM)
hbm = pl.BlockSpec(memory_space=pltpu.HBM)


def partner(x, axis, distance):
    return lax.ppermute(x, axis, [(i, i ^ distance) for i in range(lax.axis_size(axis))])


def in_hbm(array):
    return pltpu.with_memory_space_constraint(array, pltpu.HBM)


def after(array, *others):
    return lax.optimization_barrier((array, *others))[0]


def run_copies(moves):
    for move in moves:
        move.start()
    for move in moves:
        move.wait()


def lead_kernel(count, slot, field, piece, sem):
    rows = piece.shape[1]
    start = pl.multiple_of((lax.axis_index("gz") ^ slot) * rows, ROWS)
    run_copies([pltpu.make_async_copy(field.at[:, pl.ds(start, rows)], piece, sem)])


def split_kernel(count, depth, slots, field, *refs):
    pieces = refs[: len(slots)]
    last, first, ends, sems = refs[len(slots) :]
    height = field.shape[1]
    rows = height // count
    rank = lax.axis_index("gz")
    moves = [
        pltpu.make_async_copy(field.at[:, height - ROWS :], ends.at[0], sems.at[0]),
        pltpu.make_async_copy(field.at[:, :ROWS], ends.at[1], sems.at[1]),
    ]
    for index, slot in enumerate(slots):
        start = pl.multiple_of((rank ^ slot) * rows, ROWS)
        moves.append(pltpu.make_async_copy(field.at[:, pl.ds(start, rows)], pieces[index], sems.at[2 + index]))
    run_copies(moves)
    for j in range(depth):
        last[j : j + 1, :] = ends[0, j, ROWS - 1 :, :]
        first[j : j + 1, :] = ends[1, j, :1, :]


def pack_kernel(count, depth, early, later, above, below, table, march, field, bins, *refs):
    messages = refs[: count - 1]
    edges, entries, flips, *pieces, high, low, labels, sems, cut_sems = refs[count - 1 :]
    height, width = field.shape[1:]
    rows = height // count
    half = width // 2
    rank = lax.axis_index("gz")
    copies = []
    for slot in range(count):
        target = rank ^ slot
        top = pl.multiple_of(jnp.maximum(target * rows - ROWS, 0), ROWS)
        bottom = pl.multiple_of(jnp.minimum(target * rows + rows, height - ROWS), ROWS)
        start = pl.multiple_of(target * rows, ROWS)
        moves = [
            pltpu.make_async_copy(field.at[:, pl.ds(top, ROWS)], high.at[slot], sems.at[slot, 0]),
            pltpu.make_async_copy(field.at[:, pl.ds(bottom, ROWS)], low.at[slot], sems.at[slot, 1]),
        ]
        if slot:
            moves.append(
                pltpu.make_async_copy(bins.at[:, pl.ds(start, early)], labels.at[slot - 1], sems.at[slot, 2])
            )
        for move in moves:
            move.start()
        copies.append(moves)
    cuts = []
    for index, (slot, top, size) in enumerate(later):
        start = pl.multiple_of((rank ^ slot) * rows + top, ROWS)
        cuts.append(pltpu.make_async_copy(bins.at[:, pl.ds(start, size)], pieces[index], cut_sems.at[index]))
        cuts[-1].start()
    pair = pack_entries(table[...].astype(jnp.float32))
    for word in range(2):
        entries[word] = pair[word]
    for row in range(rows):
        flips[row : row + 1, :] = jnp.full((1, LANES), march[rank * rows + row], jnp.int32)
    for slot in range(count):
        target = rank ^ slot
        for move in copies[slot]:
            move.wait()
        message = messages[slot - 1] if slot else edges
        for j in range(depth):
            upper = jnp.where(target == 0, above[j : j + 1, :], high[slot, j, ROWS - 1 : ROWS, :])
            lower = jnp.where(target == count - 1, below[j : j + 1, :], low[slot, j, 0:1, :])
            for h in range(2):
                cols = slice(h * half, (h + 1) * half)
                at = 2 * depth * h + j
                message[at : at + 1, :] = upper[:, cols]
                message[at + depth : at + depth + 1, :] = lower[:, cols]
                if slot:
                    first = 4 * depth + (2 * j + h) * early
                    message[first : first + early, :] = labels[slot - 1, j, :, cols].astype(jnp.float32)
    for move in cuts:
        move.wait()


def side_kernel(count, depth, field, *refs):
    bricks = (None,) + refs[: count - 1]
    slab, own, sem = refs[count - 1 :]
    rows = slab.shape[1]
    width = field.shape[2]
    side = lax.axis_index("sx")
    start = pl.multiple_of(lax.axis_index("gz") * rows, ROWS)
    column = pl.multiple_of((1 - side) * (width - LANES), LANES)
    move = pltpu.make_async_copy(field.at[:, pl.ds(start, rows), pl.ds(column, LANES)], own, sem)
    move.start()
    for slot in range(1, count):
        for j in range(depth):
            slab[slot * depth + j] = jnp.where(
                side == 1, bricks[slot][j, :, :LANES], bricks[slot][j, :, width - LANES :]
            )
    move.wait()
    for j in range(depth):
        slab[j] = own[j]


def pack_entries(table):
    units = [1.0 / COLOUR_UNIT] * 3 + [1.0 / OPACITY_UNIT]
    rows = [
        jnp.broadcast_to((table[c : c + 1, :] * units[c]).astype(jnp.int32), (ROWS, table.shape[1])) for c in range(4)
    ]
    return rows[0] | rows[1] << HALF_WORD, rows[2] | rows[3] << HALF_WORD


def look(entries, labels):
    return jnp.take_along_axis(entries, labels, axis=1, mode="promise_in_bounds")


def low_part(words):
    return (words & ((1 << HALF_WORD) - 1)).astype(jnp.float32)


def high_part(words):
    return (words >> HALF_WORD).astype(jnp.float32)


def blend_rows(count, depth, words, back, scaled, span, shading, shaded, result, here, finish):
    rank = lax.axis_index("gz")
    tiles = result.shape[2] // LANES
    unroll = max(min(tiles // COPIES, UNROLLED // (count * depth)), 1)
    ahead = [
        [jnp.where((rank ^ other) < (rank ^ slot), 1.0, 0.0) for other in range(count)] for slot in range(count)
    ]

    def blend_tile(cols, h):
        found = [words(cell, cols, h) for cell in range(count * depth)]
        taus = [high_part(found[cell][1]) * scaled[cell, span, cols] for cell in range(count * depth)]
        inner = []
        for slot in range(count):
            sums = [taus[slot * depth]]
            for j in range(1, depth):
                sums.append(sums[-1] + taus[slot * depth + j])
            inner.append(sums)
        whole = sum(sums[-1] for sums in inner)
        sign = jnp.where(back, 1.0, -1.0)
        shift = jnp.where(back, -whole, 0.0)
        colour = [jnp.zeros((ROWS, LANES), jnp.float32) for _ in range(3)]
        for slot in range(count):
            front = sum(inner[other][-1] * ahead[slot][other] for other in range(count) if other != slot)
            reached = [front] + [front + part for part in inner[slot]]
            through = [jnp.exp2(sign * part + shift) for part in reached]
            for j in range(depth):
                cell = slot * depth + j
                weight = jnp.abs(through[j] - through[j + 1]) * shading[cell, shaded, cols]
                colour[0] = colour[0] + weight * low_part(found[cell][0])
                colour[1] = colour[1] + weight * high_part(found[cell][0])
                colour[2] = colour[2] + weight * low_part(found[cell][1])
        for c in range(3):
            result[c, here, cols] = colour[c]
        result[3, here, cols] = 1.0 - jnp.exp2(-whole)

    quarter = tiles // COPIES
    for part in range(COPIES):
        h = 2 * part // COPIES
        if unroll == quarter:
            for tile in range(part * quarter, (part + 1) * quarter):
                blend_tile(slice(tile * LANES, (tile + 1) * LANES), h)
        else:

            def tile_step(step, _, part=part, h=h):
                for tile in range(unroll):
                    left = (part * quarter + step * unroll + tile) * LANES
                    blend_tile(pl.ds(pl.multiple_of(left, LANES), LANES), h)
                return 0

            lax.fori_loop(0, quarter // unroll, tile_step, 0)
        finish(part)


def copy_out(result, image, sems, top, start):
    columns = result.shape[2] // COPIES
    return [
        pltpu.make_async_copy(
            result.at[:, top : top + ROWS, part * columns : (part + 1) * columns],
            image.at[:, start + top : start + top + ROWS, part * columns : (part + 1) * columns],
            sems.at[top // ROWS, part],
        )
        for part in range(COPIES)
    ]


def shade_tile(ext, at, top, width, dy_of, store):
    here = slice(ROWS + top, 2 * ROWS + top)
    lane = lax.broadcasted_iota(jnp.int32, (ROWS, LANES), 1)
    first = lane == 0
    last = lane == LANES - 1
    tiles = [ext[at + 1, here, left : left + LANES] for left in range(0, width + 2 * LANES, LANES)]
    toward = [pltpu.roll(tile, LANES - 1, 1) for tile in tiles]
    away = [pltpu.roll(tile, 1, 1) for tile in tiles]
    for c in range(1, width // LANES + 1):
        cols = slice(c * LANES, (c + 1) * LANES)
        dx = jnp.where(last, toward[c + 1], toward[c]) - jnp.where(first, away[c - 1], away[c])
        dy = dy_of(
            c - 1,
            ext[at + 1, ROWS + top + 1 : 2 * ROWS + top + 1, cols]
            - ext[at + 1, ROWS + top - 1 : 2 * ROWS + top - 1, cols],
        )
        dz = ext[at + 2, here, cols] - ext[at, here, cols]
        facing = jnp.abs((0.5 * light_x) * dx + (0.5 * light_y) * dy + (0.5 * light_z) * dz)
        square = 0.25 * (dx * dx + dy * dy + dz * dz) + 1.0
        store(c - 1, 0.3 * COLOUR_UNIT + (0.7 * COLOUR_UNIT) * facing * lax.rsqrt(square))


def inner_kernel(count, depth, field, edges, beside, entries, *refs):
    parts = len(refs) - (count - 1) - 7
    bricks = refs[: count - 1]
    own_bins = refs[count - 1 : count - 1 + parts]
    ext, scaled, inner, known, token, own_brick, sem = refs[count - 1 + parts :]
    rows, width = scaled.shape[1:]
    half = width // 2
    total = count * depth
    rank = lax.axis_index("gz")
    side = lax.axis_index("sx")
    inside = slice(ROWS, ROWS + rows)
    move = pltpu.make_async_copy(field.at[:, pl.ds(pl.multiple_of(rank * rows, ROWS), rows)], own_brick, sem)
    move.start()
    bricks = (own_brick, *bricks)
    zero_plane = jnp.zeros((rows, width), jnp.float32)
    zero_row = jnp.zeros((ROWS, width), jnp.float32)
    ext[0, inside, LANES : LANES + width] = zero_plane
    ext[total + 1, inside, LANES : LANES + width] = zero_plane
    for slot in reversed(range(count)):
        if slot == 0:
            move.wait()
        for j in range(depth):
            at = (rank ^ slot) * depth + j
            plane = bricks[slot][j]
            scaled[slot * depth + j] = plane * (OPACITY_UNIT * LOG2_E)
            ext[at + 1, inside, LANES : LANES + width] = plane
            ext[at + 1, :ROWS, LANES : LANES + width] = zero_row
            ext[at + 1, ROWS + rows :, LANES : LANES + width] = zero_row
            if slot == 0:
                for h in range(2):
                    cols = slice(LANES + h * half, LANES + (h + 1) * half)
                    row = 2 * depth * h + j
                    ext[at + 1, ROWS - 1 : ROWS, cols] = edges[row : row + 1, :]
                    ext[at + 1, ROWS + rows : ROWS + rows + 1, cols] = edges[row + depth : row + depth + 1, :]
            column = beside[slot * depth + j]
            ext[at + 1, inside, :LANES] = jnp.where(side == 1, column, 0.0)
            ext[at + 1, inside, LANES + width :] = jnp.where(side == 0, column, 0.0)
    pair = (entries[0], entries[1])
    start = 0
    for part in own_bins:
        size = part.shape[1]
        for j in range(depth):
            for top in range(0, size, ROWS):
                for left in range(0, width, LANES):
                    cols = slice(left, left + LANES)
                    labels = part[j, top : top + ROWS, cols]
                    for word in range(2):
                        known[word, j, start + top : start + top + ROWS, cols] = look(pair[word], labels)
        start += size

    def plane_step(cell, _):
        at = (rank ^ (cell // depth)) * depth + cell % depth
        for top in range(ROWS, rows - ROWS, ROWS):

            def store(c, value, top=top):
                inner[cell, top - ROWS : top, c * LANES : (c + 1) * LANES] = value

            shade_tile(ext, at, top, width, lambda c, dy: dy, store)
        return 0

    if rows > 2 * ROWS:
        lax.fori_loop(0, total, plane_step, 0)
    else:
        inner[...] = jnp.zeros_like(inner)
    token[...] = jnp.zeros_like(token)


def outer_kernel(count, depth, entries, flips, ext, scaled, inner, known, *refs):
    messages = refs[: count - 1]
    outer, image, result, sems = refs[count - 1 :]
    rows, width = scaled.shape[1:]
    early = result.shape[1]
    half = width // 2
    rank = lax.axis_index("gz")
    pair = (entries[0], entries[1])
    row_of = lax.broadcasted_iota(jnp.int32, (ROWS, LANES), 0)

    def shade(top):
        for cell in range(count * depth):
            slot, j = divmod(cell, depth)
            at = (rank ^ slot) * depth + j

            def dy_of(c, dy, slot=slot, j=j):
                if slot == 0:
                    return dy
                h, left = c * LANES // half, c * LANES % half
                row = 2 * depth * h + j
                cols = slice(left, left + LANES)
                if top == 0:
                    dy = dy - jnp.where(row_of == 0, messages[slot - 1][row : row + 1, cols], 0.0)
                if top == rows - ROWS:
                    beyond = messages[slot - 1][row + depth : row + depth + 1, cols]
                    dy = dy + jnp.where(row_of == ROWS - 1, beyond, 0.0)
                return dy

            def store(c, value, cell=cell):
                place = 0 if top == 0 else ROWS
                outer[cell, place : place + ROWS, c * LANES : (c + 1) * LANES] = value

            shade_tile(ext, at, top, width, dy_of, store)

    shade(0)
    copies = []
    for top in range(0, early, ROWS):
        here = slice(top, top + ROWS)

        def words(cell, cols, h, top=top):
            slot, j = divmod(cell, depth)
            if slot == 0:
                return tuple(known[word, j, top : top + ROWS, cols] for word in range(2))
            left = cols.start - h * half
            left = pl.ds(left if isinstance(left, int) else pl.multiple_of(left, LANES), LANES)
            row = 4 * depth + (2 * j + h) * early + top
            labels = messages[slot - 1][row : row + ROWS, left].astype(jnp.int32)
            return look(pair[0], labels), look(pair[1], labels)

        parts = copy_out(result, image, sems, top, 0)
        shading, shaded = (outer, slice(0, ROWS)) if top == 0 else (inner, slice(top - ROWS, top))
        blend_rows(
            count, depth, words, flips[here, :] == 1, scaled, here, shading, shaded, result, here,
            lambda part, parts=parts: parts[part].start(),
        )
        copies += parts
    if rows > ROWS:
        shade(rows - ROWS)
    for move in copies:
        move.wait()


def look_kernel(depth, entries, brick, found):
    rows, width = found.shape[2:]
    for j in range(depth):
        for top in range(0, rows, ROWS):
            for left in range(0, width, LANES):
                at = (slice(top, top + ROWS), slice(left, left + LANES))
                labels = brick[(j, *at)]
                for word in range(2):
                    found[(word, j, *at)] = look(entries[word], labels)


def blend_kernel(count, depth, start, late, lead, entries, flips, scaled, shading, known, found, *refs):
    bricks = refs[: count - 2]
    image, result, sems = refs[-3:]
    rows = result.shape[1]
    pair = (entries[0], entries[1])
    unknown = [slot for slot in range(1, count) if slot != lead]
    copies = []
    for top in range(0, rows, ROWS):
        here = slice(top, top + ROWS)
        span = slice(start + top, start + top + ROWS)
        inner = start + top + ROWS < scaled.shape[1]
        shaded = slice(start + top - ROWS, start + top) if inner else slice(ROWS, 2 * ROWS)

        def words(cell, cols, h, here=here, span=span, top=top):
            slot, j = divmod(cell, depth)
            if slot == 0:
                return tuple(known[word, j, span, cols] for word in range(2))
            if slot == lead:
                begin = start + top - late
                return tuple(found[word, j, begin : begin + ROWS, cols] for word in range(2))
            labels = bricks[unknown.index(slot)][j, here, cols]
            return look(pair[0], labels), look(pair[1], labels)

        parts = copy_out(result, image, sems, top, start)
        blend_rows(
            count, depth, words, flips[span, :] == 1, scaled, span, shading, shaded, result, here,
            lambda part, parts=parts: parts[part].start(),
        )
        copies += parts
    for move in copies:
        move.wait()


def shards(field, bins, table, march_order):
    depth, height, width = field.shape
    count = lax.axis_size("gz")
    rank = lax.axis_index("gz").astype(jnp.int32)
    rows = height // count
    total = count * depth
    half = width // 2
    slots = range(count)
    partners = sorted(range(1, count), key=lambda slot: (-slot.bit_count(), slot))
    lead, *others = partners
    params = pltpu.CompilerParams(vmem_limit_bytes=VMEM_LIMIT)

    def cost(cells):
        return pl.CostEstimate(flops=20 * cells, bytes_accessed=8 * cells, transcendentals=cells)

    done = {}
    order = {"message": lambda index: [("field", 0)], "bins": lambda index: [("message", index), "inner"]}

    def send(name, array, slot):
        index = partners.index(slot)
        waits = [done[key] for key in order.get(name, lambda index: ())(index)]
        done[name, index] = partner(after(array, *waits), "gz", slot)
        return done[name, index]

    bricks = {}
    sent = pl.pallas_call(
        functools.partial(lead_kernel, count, lead),
        out_shape=pltpu.VMEM((depth, rows, width), jnp.float32),
        in_specs=[hbm],
        out_specs=vmem,
        scratch_shapes=[pltpu.SemaphoreType.DMA],
        compiler_params=params,
        cost_estimate=cost(depth * rows * width),
        name="lead",
    )(in_hbm(field))
    bricks[lead] = send("field", sent, lead)

    *pieces, last, first = pl.pallas_call(
        functools.partial(split_kernel, count, depth, others),
        out_shape=[pltpu.VMEM((depth, rows, width), jnp.float32)] * len(others)
        + [pltpu.VMEM((depth, width), jnp.float32)] * 2,
        in_specs=[hbm],
        out_specs=[vmem] * count,
        scratch_shapes=[pltpu.VMEM((2, depth, ROWS, width), jnp.float32), pltpu.SemaphoreType.DMA((count,))],
        compiler_params=params,
        cost_estimate=cost(depth * height * width),
        name="split",
    )(in_hbm(after(field, sent)))
    for slot, sent in zip(others, pieces):
        bricks[slot] = send("field", sent, slot)

    forward = [(i, i + 1) for i in range(lax.axis_size("sy") - 1)]
    backward = [(target, origin) for origin, target in forward]
    above = lax.ppermute(last, "sy", forward)
    below = lax.ppermute(first, "sy", backward)

    early = max(rows // 2 // ROWS, 1) * ROWS
    late = rows - early
    later = []
    if late:
        later = [(0, 0, rows), (lead, early, late)]
        pieces = [(early, late - ROWS), (rows - ROWS, ROWS)] if late > ROWS else [(early, late)]
        later += [(slot, top, size) for top, size in pieces for slot in others]
    else:
        pieces = []
        later = [(0, 0, rows)]
    message_rows = 4 * depth + 2 * depth * early
    packed = pl.pallas_call(
        functools.partial(pack_kernel, count, depth, early, later),
        out_shape=[pltpu.VMEM((message_rows, half), jnp.float32)] * (count - 1)
        + [
            jax.ShapeDtypeStruct((4 * depth, half), jnp.float32),
            jax.ShapeDtypeStruct((2, ROWS, table.shape[1]), jnp.int32),
            jax.ShapeDtypeStruct((rows, LANES), jnp.int32),
        ]
        + [jax.ShapeDtypeStruct((depth, size, width), jnp.int32) for _, _, size in later],
        in_specs=[vmem, vmem, vmem, pl.BlockSpec(memory_space=pltpu.SMEM), hbm, hbm],
        out_specs=[vmem] * (count + 2 + len(later)),
        scratch_shapes=[
            pltpu.VMEM((count, depth, ROWS, width), jnp.float32),
            pltpu.VMEM((count, depth, ROWS, width), jnp.float32),
            pltpu.VMEM((count - 1, depth, early, width), jnp.int32),
            pltpu.SemaphoreType.DMA((count, 3)),
            pltpu.SemaphoreType.DMA((len(later),)),
        ],
        compiler_params=params,
        cost_estimate=cost(depth * height * width),
        name="pack",
    )(above, below, table, march_order, in_hbm(field), in_hbm(bins))
    messages = {}
    for slot in partners:
        messages[slot] = send("message", packed[slot - 1], slot)
    edges, entries, flips = packed[count - 1 : count + 2]
    cuts = packed[count + 2 :]

    slab = pl.pallas_call(
        functools.partial(side_kernel, count, depth),
        out_shape=pltpu.VMEM((total, rows, LANES), jnp.float32),
        in_specs=[hbm] + [vmem] * (count - 1),
        out_specs=vmem,
        scratch_shapes=[pltpu.VMEM((depth, rows, LANES), jnp.float32), pltpu.SemaphoreType.DMA],
        compiler_params=params,
        cost_estimate=cost(total * rows * LANES),
        name="side",
    )(in_hbm(field), *[bricks[slot] for slot in slots[1:]])
    beside = partner(slab, "sx", 1)

    ext, scaled, inner, known, token = pl.pallas_call(
        functools.partial(inner_kernel, count, depth),
        out_shape=(
            pltpu.VMEM((total + 2, rows + 2 * ROWS, width + 2 * LANES), jnp.float32),
            pltpu.VMEM((total, rows, width), jnp.float32),
            pltpu.VMEM((total, max(rows - 2 * ROWS, ROWS), width), jnp.float32),
            pltpu.VMEM((2, depth, rows, width), jnp.int32),
            jax.ShapeDtypeStruct((ROWS, LANES), jnp.float32),
        ),
        in_specs=[hbm] + [vmem] * (count + 3),
        out_specs=[vmem] * 5,
        scratch_shapes=[pltpu.VMEM((depth, rows, width), jnp.float32), pltpu.SemaphoreType.DMA],
        compiler_params=params,
        cost_estimate=cost(total * rows * width),
        name="inner",
    )(in_hbm(field), edges, beside, entries, *[bricks[slot] for slot in slots[1:]], cuts[0])
    done["inner"] = token

    image_shape = jax.ShapeDtypeStruct((4, rows, width), jnp.float32)
    outer, image = pl.pallas_call(
        functools.partial(outer_kernel, count, depth),
        out_shape=(pltpu.VMEM((total, 2 * ROWS, width), jnp.float32), image_shape),
        in_specs=[vmem] * (count + 5),
        out_specs=(vmem, hbm),
        scratch_shapes=[
            pltpu.VMEM((4, early, width), jnp.float32),
            pltpu.SemaphoreType.DMA((early // ROWS, COPIES)),
        ],
        compiler_params=params,
        cost_estimate=cost(total * rows * width),
        name="outer",
    )(entries, flips, ext, scaled, inner, known, *[messages[slot] for slot in slots[1:]])
    if not late:
        return image

    arrived = [send("bins", cut, slot) for (slot, _, _), cut in zip(later[1:], cuts[1:])]
    found = pl.pallas_call(
        functools.partial(look_kernel, depth),
        out_shape=pltpu.VMEM((2, depth, late, width), jnp.int32),
        in_specs=[vmem] * 2,
        out_specs=vmem,
        compiler_params=params,
        cost_estimate=cost(depth * late * width),
        name="look",
    )(entries, arrived[0])
    for index, (top, size) in enumerate(pieces):
        labels = arrived[1 + index * len(others) : 1 + (index + 1) * len(others)]
        labels = [labels[others.index(slot)] for slot in sorted(others)]
        shading = outer if top + size == rows else inner
        operands = [entries, flips, scaled, shading, known, found, *labels, image]
        image = pl.pallas_call(
            functools.partial(blend_kernel, count, depth, top, early, lead),
            out_shape=image_shape,
            in_specs=[vmem] * (len(operands) - 1) + [hbm],
            out_specs=hbm,
            scratch_shapes=[
                pltpu.VMEM((4, size, width), jnp.float32),
                pltpu.SemaphoreType.DMA((size // ROWS, COPIES)),
            ],
            input_output_aliases={len(operands) - 1: 0},
            compiler_params=params,
            cost_estimate=cost(total * size * width),
            name="blend",
        )(*operands)
    return image


def solution(mesh):
    placed = (P("gz", "sy", "sx"), P("gz", "sy", "sx"), P(), P("sy"))
    return jax.shard_map(
        shards, mesh=mesh, in_specs=placed, out_specs=P(None, ("sy", "gz"), "sx"), check_vma=False
    )
```

```python
import functools

import jax
import jax.numpy as jnp
from jax import lax
from jax.experimental import pallas as pl
from jax.experimental.pallas import tpu as pltpu
from jax.sharding import PartitionSpec as P

light_x = 0.36
light_y = 0.48
light_z = 0.8
LANES = 128
ROWS = 8
COLOUR_UNIT = 2.0**-12
OPACITY_UNIT = 2.0**-13
HALF_WORD = 16
LOG2_E = 1.4426950408889634
UNROLLED = 32
COPIES = 4
VMEM_LIMIT = 40 * 1024 * 1024

vmem = pl.BlockSpec(memory_space=pltpu.VMEM)
hbm = pl.BlockSpec(memory_space=pltpu.HBM)


def partner(x, axis, distance):
    return lax.ppermute(x, axis, [(i, i ^ distance) for i in range(lax.axis_size(axis))])


def in_hbm(array):
    return pltpu.with_memory_space_constraint(array, pltpu.HBM)


def after(array, *others):
    return lax.optimization_barrier((array, *others))[0]


def run_copies(moves):
    for move in moves:
        move.start()
    for move in moves:
        move.wait()


def lead_kernel(count, slot, field, piece, sem):
    rows = piece.shape[1]
    start = pl.multiple_of((lax.axis_index("gz") ^ slot) * rows, ROWS)
    run_copies([pltpu.make_async_copy(field.at[:, pl.ds(start, rows)], piece, sem)])


def split_kernel(count, depth, slots, field, *refs):
    pieces = refs[: len(slots)]
    last, first, ends, sems = refs[len(slots) :]
    height = field.shape[1]
    rows = height // count
    rank = lax.axis_index("gz")
    moves = [
        pltpu.make_async_copy(field.at[:, height - ROWS :], ends.at[0], sems.at[0]),
        pltpu.make_async_copy(field.at[:, :ROWS], ends.at[1], sems.at[1]),
    ]
    for index, slot in enumerate(slots):
        start = pl.multiple_of((rank ^ slot) * rows, ROWS)
        moves.append(pltpu.make_async_copy(field.at[:, pl.ds(start, rows)], pieces[index], sems.at[2 + index]))
    run_copies(moves)
    for j in range(depth):
        last[j : j + 1, :] = ends[0, j, ROWS - 1 :, :]
        first[j : j + 1, :] = ends[1, j, :1, :]


def pack_kernel(count, depth, early, later, above, below, table, march, field, bins, *refs):
    messages = refs[: count - 1]
    edges, entries, flips, *pieces, high, low, labels, sems, cut_sems = refs[count - 1 :]
    height, width = field.shape[1:]
    rows = height // count
    half = width // 2
    rank = lax.axis_index("gz")
    copies = []
    for slot in range(count):
        target = rank ^ slot
        top = pl.multiple_of(jnp.maximum(target * rows - ROWS, 0), ROWS)
        bottom = pl.multiple_of(jnp.minimum(target * rows + rows, height - ROWS), ROWS)
        start = pl.multiple_of(target * rows, ROWS)
        moves = [
            pltpu.make_async_copy(field.at[:, pl.ds(top, ROWS)], high.at[slot], sems.at[slot, 0]),
            pltpu.make_async_copy(field.at[:, pl.ds(bottom, ROWS)], low.at[slot], sems.at[slot, 1]),
        ]
        if slot:
            moves.append(
                pltpu.make_async_copy(bins.at[:, pl.ds(start, early)], labels.at[slot - 1], sems.at[slot, 2])
            )
        for move in moves:
            move.start()
        copies.append(moves)
    cuts = []
    for index, (slot, top, size) in enumerate(later):
        start = pl.multiple_of((rank ^ slot) * rows + top, ROWS)
        cuts.append(pltpu.make_async_copy(bins.at[:, pl.ds(start, size)], pieces[index], cut_sems.at[index]))
        cuts[-1].start()
    pair = pack_entries(table[...].astype(jnp.float32))
    for word in range(2):
        entries[word] = pair[word]
    for row in range(rows):
        flips[row : row + 1, :] = jnp.full((1, LANES), march[rank * rows + row], jnp.int32)
    for slot in range(count):
        target = rank ^ slot
        for move in copies[slot]:
            move.wait()
        message = messages[slot - 1] if slot else edges
        for j in range(depth):
            upper = jnp.where(target == 0, above[j : j + 1, :], high[slot, j, ROWS - 1 : ROWS, :])
            lower = jnp.where(target == count - 1, below[j : j + 1, :], low[slot, j, 0:1, :])
            for h in range(2):
                cols = slice(h * half, (h + 1) * half)
                at = 2 * depth * h + j
                message[at : at + 1, :] = upper[:, cols]
                message[at + depth : at + depth + 1, :] = lower[:, cols]
                if slot:
                    first = 4 * depth + (2 * j + h) * early
                    message[first : first + early, :] = labels[slot - 1, j, :, cols].astype(jnp.float32)
    for move in cuts:
        move.wait()


def side_kernel(count, depth, field, *refs):
    bricks = (None,) + refs[: count - 1]
    slab, own, sem = refs[count - 1 :]
    rows = slab.shape[1]
    width = field.shape[2]
    side = lax.axis_index("sx")
    start = pl.multiple_of(lax.axis_index("gz") * rows, ROWS)
    column = pl.multiple_of((1 - side) * (width - LANES), LANES)
    move = pltpu.make_async_copy(field.at[:, pl.ds(start, rows), pl.ds(column, LANES)], own, sem)
    move.start()
    for slot in range(1, count):
        for j in range(depth):
            slab[slot * depth + j] = jnp.where(
                side == 1, bricks[slot][j, :, :LANES], bricks[slot][j, :, width - LANES :]
            )
    move.wait()
    for j in range(depth):
        slab[j] = own[j]


def pack_entries(table):
    units = [1.0 / COLOUR_UNIT] * 3 + [1.0 / OPACITY_UNIT]
    rows = [
        jnp.broadcast_to((table[c : c + 1, :] * units[c]).astype(jnp.int32), (ROWS, table.shape[1])) for c in range(4)
    ]
    return rows[0] | rows[1] << HALF_WORD, rows[2] | rows[3] << HALF_WORD


def look(entries, labels):
    return jnp.take_along_axis(entries, labels, axis=1, mode="promise_in_bounds")


def low_part(words):
    return (words & ((1 << HALF_WORD) - 1)).astype(jnp.float32)


def high_part(words):
    return (words >> HALF_WORD).astype(jnp.float32)


def blend_rows(count, depth, words, back, scaled, span, shading, shaded, result, here, finish):
    rank = lax.axis_index("gz")
    tiles = result.shape[2] // LANES
    unroll = max(min(tiles // COPIES, UNROLLED // (count * depth)), 1)
    ahead = [
        [jnp.where((rank ^ other) < (rank ^ slot), 1.0, 0.0) for other in range(count)] for slot in range(count)
    ]

    def blend_tile(cols, h):
        found = [words(cell, cols, h) for cell in range(count * depth)]
        taus = [high_part(found[cell][1]) * scaled[cell, span, cols] for cell in range(count * depth)]
        inner = []
        for slot in range(count):
            sums = [taus[slot * depth]]
            for j in range(1, depth):
                sums.append(sums[-1] + taus[slot * depth + j])
            inner.append(sums)
        whole = sum(sums[-1] for sums in inner)
        sign = jnp.where(back, 1.0, -1.0)
        shift = jnp.where(back, -whole, 0.0)
        colour = [jnp.zeros((ROWS, LANES), jnp.float32) for _ in range(3)]
        for slot in range(count):
            front = sum(inner[other][-1] * ahead[slot][other] for other in range(count) if other != slot)
            reached = [front] + [front + part for part in inner[slot]]
            through = [jnp.exp2(sign * part + shift) for part in reached]
            for j in range(depth):
                cell = slot * depth + j
                weight = jnp.abs(through[j] - through[j + 1]) * shading[cell, shaded, cols]
                colour[0] = colour[0] + weight * low_part(found[cell][0])
                colour[1] = colour[1] + weight * high_part(found[cell][0])
                colour[2] = colour[2] + weight * low_part(found[cell][1])
        for c in range(3):
            result[c, here, cols] = colour[c]
        result[3, here, cols] = 1.0 - jnp.exp2(-whole)

    quarter = tiles // COPIES
    for part in range(COPIES):
        h = 2 * part // COPIES
        if unroll == quarter:
            for tile in range(part * quarter, (part + 1) * quarter):
                blend_tile(slice(tile * LANES, (tile + 1) * LANES), h)
        else:

            def tile_step(step, _, part=part, h=h):
                for tile in range(unroll):
                    left = (part * quarter + step * unroll + tile) * LANES
                    blend_tile(pl.ds(pl.multiple_of(left, LANES), LANES), h)
                return 0

            lax.fori_loop(0, quarter // unroll, tile_step, 0)
        finish(part)


def copy_out(result, image, sems, top, start):
    columns = result.shape[2] // COPIES
    return [
        pltpu.make_async_copy(
            result.at[:, top : top + ROWS, part * columns : (part + 1) * columns],
            image.at[:, start + top : start + top + ROWS, part * columns : (part + 1) * columns],
            sems.at[top // ROWS, part],
        )
        for part in range(COPIES)
    ]


def shade_tile(ext, at, top, width, dy_of, store):
    here = slice(ROWS + top, 2 * ROWS + top)
    lane = lax.broadcasted_iota(jnp.int32, (ROWS, LANES), 1)
    first = lane == 0
    last = lane == LANES - 1
    tiles = [ext[at + 1, here, left : left + LANES] for left in range(0, width + 2 * LANES, LANES)]
    toward = [pltpu.roll(tile, LANES - 1, 1) for tile in tiles]
    away = [pltpu.roll(tile, 1, 1) for tile in tiles]
    for c in range(1, width // LANES + 1):
        cols = slice(c * LANES, (c + 1) * LANES)
        dx = jnp.where(last, toward[c + 1], toward[c]) - jnp.where(first, away[c - 1], away[c])
        dy = dy_of(
            c - 1,
            ext[at + 1, ROWS + top + 1 : 2 * ROWS + top + 1, cols]
            - ext[at + 1, ROWS + top - 1 : 2 * ROWS + top - 1, cols],
        )
        dz = ext[at + 2, here, cols] - ext[at, here, cols]
        facing = jnp.abs((0.5 * light_x) * dx + (0.5 * light_y) * dy + (0.5 * light_z) * dz)
        square = 0.25 * (dx * dx + dy * dy + dz * dz) + 1.0
        store(c - 1, 0.3 * COLOUR_UNIT + (0.7 * COLOUR_UNIT) * facing * lax.rsqrt(square))


def inner_kernel(count, depth, field, edges, beside, entries, *refs):
    parts = len(refs) - (count - 1) - 7
    bricks = refs[: count - 1]
    own_bins = refs[count - 1 : count - 1 + parts]
    ext, scaled, inner, known, token, own_brick, sem = refs[count - 1 + parts :]
    rows, width = scaled.shape[1:]
    half = width // 2
    total = count * depth
    rank = lax.axis_index("gz")
    side = lax.axis_index("sx")
    inside = slice(ROWS, ROWS + rows)
    move = pltpu.make_async_copy(field.at[:, pl.ds(pl.multiple_of(rank * rows, ROWS), rows)], own_brick, sem)
    move.start()
    bricks = (own_brick, *bricks)
    zero_plane = jnp.zeros((rows, width), jnp.float32)
    zero_row = jnp.zeros((ROWS, width), jnp.float32)
    ext[0, inside, LANES : LANES + width] = zero_plane
    ext[total + 1, inside, LANES : LANES + width] = zero_plane
    for slot in reversed(range(count)):
        if slot == 0:
            move.wait()
        for j in range(depth):
            at = (rank ^ slot) * depth + j
            plane = bricks[slot][j]
            scaled[slot * depth + j] = plane * (OPACITY_UNIT * LOG2_E)
            ext[at + 1, inside, LANES : LANES + width] = plane
            ext[at + 1, :ROWS, LANES : LANES + width] = zero_row
            ext[at + 1, ROWS + rows :, LANES : LANES + width] = zero_row
            if slot == 0:
                for h in range(2):
                    cols = slice(LANES + h * half, LANES + (h + 1) * half)
                    row = 2 * depth * h + j
                    ext[at + 1, ROWS - 1 : ROWS, cols] = edges[row : row + 1, :]
                    ext[at + 1, ROWS + rows : ROWS + rows + 1, cols] = edges[row + depth : row + depth + 1, :]
            column = beside[slot * depth + j]
            ext[at + 1, inside, :LANES] = jnp.where(side == 1, column, 0.0)
            ext[at + 1, inside, LANES + width :] = jnp.where(side == 0, column, 0.0)
    pair = (entries[0], entries[1])
    start = 0
    for part in own_bins:
        size = part.shape[1]
        for j in range(depth):
            for top in range(0, size, ROWS):
                for left in range(0, width, LANES):
                    cols = slice(left, left + LANES)
                    labels = part[j, top : top + ROWS, cols]
                    for word in range(2):
                        known[word, j, start + top : start + top + ROWS, cols] = look(pair[word], labels)
        start += size

    def plane_step(cell, _):
        at = (rank ^ (cell // depth)) * depth + cell % depth
        for top in range(ROWS, rows - ROWS, ROWS):

            def store(c, value, top=top):
                inner[cell, top - ROWS : top, c * LANES : (c + 1) * LANES] = value

            shade_tile(ext, at, top, width, lambda c, dy: dy, store)
        return 0

    if rows > 2 * ROWS:
        lax.fori_loop(0, total, plane_step, 0)
    else:
        inner[...] = jnp.zeros_like(inner)
    token[...] = jnp.zeros_like(token)


def outer_kernel(count, depth, entries, flips, ext, scaled, inner, known, *refs):
    messages = refs[: count - 1]
    outer, image, result, sems = refs[count - 1 :]
    rows, width = scaled.shape[1:]
    early = result.shape[1]
    half = width // 2
    rank = lax.axis_index("gz")
    pair = (entries[0], entries[1])
    row_of = lax.broadcasted_iota(jnp.int32, (ROWS, LANES), 0)

    def shade(top):
        for cell in range(count * depth):
            slot, j = divmod(cell, depth)
            at = (rank ^ slot) * depth + j

            def dy_of(c, dy, slot=slot, j=j):
                if slot == 0:
                    return dy
                h, left = c * LANES // half, c * LANES % half
                row = 2 * depth * h + j
                cols = slice(left, left + LANES)
                if top == 0:
                    dy = dy - jnp.where(row_of == 0, messages[slot - 1][row : row + 1, cols], 0.0)
                if top == rows - ROWS:
                    beyond = messages[slot - 1][row + depth : row + depth + 1, cols]
                    dy = dy + jnp.where(row_of == ROWS - 1, beyond, 0.0)
                return dy

            def store(c, value, cell=cell):
                place = 0 if top == 0 else ROWS
                outer[cell, place : place + ROWS, c * LANES : (c + 1) * LANES] = value

            shade_tile(ext, at, top, width, dy_of, store)

    shade(0)
    copies = []
    for top in range(0, early, ROWS):
        here = slice(top, top + ROWS)

        def words(cell, cols, h, top=top):
            slot, j = divmod(cell, depth)
            if slot == 0:
                return tuple(known[word, j, top : top + ROWS, cols] for word in range(2))
            left = cols.start - h * half
            left = pl.ds(left if isinstance(left, int) else pl.multiple_of(left, LANES), LANES)
            row = 4 * depth + (2 * j + h) * early + top
            labels = messages[slot - 1][row : row + ROWS, left].astype(jnp.int32)
            return look(pair[0], labels), look(pair[1], labels)

        parts = copy_out(result, image, sems, top, 0)
        shading, shaded = (outer, slice(0, ROWS)) if top == 0 else (inner, slice(top - ROWS, top))
        blend_rows(
            count, depth, words, flips[here, :] == 1, scaled, here, shading, shaded, result, here,
            lambda part, parts=parts: parts[part].start(),
        )
        copies += parts
    if rows > ROWS:
        shade(rows - ROWS)
    for move in copies:
        move.wait()


def look_kernel(depth, entries, brick, found):
    rows, width = found.shape[2:]
    for j in range(depth):
        for top in range(0, rows, ROWS):
            for left in range(0, width, LANES):
                at = (slice(top, top + ROWS), slice(left, left + LANES))
                labels = brick[(j, *at)]
                for word in range(2):
                    found[(word, j, *at)] = look(entries[word], labels)


def blend_kernel(count, depth, start, late, lead, entries, flips, scaled, shading, known, found, *refs):
    bricks = refs[: count - 2]
    image, result, sems = refs[-3:]
    rows = result.shape[1]
    pair = (entries[0], entries[1])
    unknown = [slot for slot in range(1, count) if slot != lead]
    copies = []
    for top in range(0, rows, ROWS):
        here = slice(top, top + ROWS)
        span = slice(start + top, start + top + ROWS)
        inner = start + top + ROWS < scaled.shape[1]
        shaded = slice(start + top - ROWS, start + top) if inner else slice(ROWS, 2 * ROWS)

        def words(cell, cols, h, here=here, span=span, top=top):
            slot, j = divmod(cell, depth)
            if slot == 0:
                return tuple(known[word, j, span, cols] for word in range(2))
            if slot == lead:
                begin = start + top - late
                return tuple(found[word, j, begin : begin + ROWS, cols] for word in range(2))
            labels = bricks[unknown.index(slot)][j, here, cols]
            return look(pair[0], labels), look(pair[1], labels)

        parts = copy_out(result, image, sems, top, start)
        blend_rows(
            count, depth, words, flips[span, :] == 1, scaled, span, shading, shaded, result, here,
            lambda part, parts=parts: parts[part].start(),
        )
        copies += parts
    for move in copies:
        move.wait()


def shards(field, bins, table, march_order):
    depth, height, width = field.shape
    count = lax.axis_size("gz")
    rank = lax.axis_index("gz").astype(jnp.int32)
    rows = height // count
    total = count * depth
    half = width // 2
    slots = range(count)
    partners = sorted(range(1, count), key=lambda slot: (-slot.bit_count(), slot))
    lead, *others = partners
    params = pltpu.CompilerParams(vmem_limit_bytes=VMEM_LIMIT)

    def cost(cells):
        return pl.CostEstimate(flops=20 * cells, bytes_accessed=8 * cells, transcendentals=cells)

    done = {}
    order = {"message": lambda index: [("field", 0)], "bins": lambda index: [("message", 0), "inner"]}

    def send(name, array, slot):
        index = partners.index(slot)
        waits = [done[key] for key in order.get(name, lambda index: ())(index)]
        done[name, index] = partner(after(array, *waits), "gz", slot)
        return done[name, index]

    bricks = {}
    sent = pl.pallas_call(
        functools.partial(lead_kernel, count, lead),
        out_shape=pltpu.VMEM((depth, rows, width), jnp.float32),
        in_specs=[hbm],
        out_specs=vmem,
        scratch_shapes=[pltpu.SemaphoreType.DMA],
        compiler_params=params,
        cost_estimate=cost(depth * rows * width),
        name="lead",
    )(in_hbm(field))
    bricks[lead] = send("field", sent, lead)

    *pieces, last, first = pl.pallas_call(
        functools.partial(split_kernel, count, depth, others),
        out_shape=[pltpu.VMEM((depth, rows, width), jnp.float32)] * len(others)
        + [pltpu.VMEM((depth, width), jnp.float32)] * 2,
        in_specs=[hbm],
        out_specs=[vmem] * count,
        scratch_shapes=[pltpu.VMEM((2, depth, ROWS, width), jnp.float32), pltpu.SemaphoreType.DMA((count,))],
        compiler_params=params,
        cost_estimate=cost(depth * height * width),
        name="split",
    )(in_hbm(after(field, sent)))
    for slot, sent in zip(others, pieces):
        bricks[slot] = send("field", sent, slot)

    forward = [(i, i + 1) for i in range(lax.axis_size("sy") - 1)]
    backward = [(target, origin) for origin, target in forward]
    above = lax.ppermute(last, "sy", forward)
    below = lax.ppermute(first, "sy", backward)

    early = max(rows - ROWS, ROWS)
    late = rows - early
    later = []
    if late:
        later = [(0, 0, rows), (lead, early, late)]
        pieces = [(early, late - ROWS), (rows - ROWS, ROWS)] if late > ROWS else [(early, late)]
        later += [(slot, top, size) for top, size in pieces for slot in others]
    else:
        pieces = []
        later = [(0, 0, rows)]
    message_rows = 4 * depth + 2 * depth * early
    packed = pl.pallas_call(
        functools.partial(pack_kernel, count, depth, early, later),
        out_shape=[pltpu.VMEM((message_rows, half), jnp.float32)] * (count - 1)
        + [
            jax.ShapeDtypeStruct((4 * depth, half), jnp.float32),
            jax.ShapeDtypeStruct((2, ROWS, table.shape[1]), jnp.int32),
            jax.ShapeDtypeStruct((rows, LANES), jnp.int32),
        ]
        + [jax.ShapeDtypeStruct((depth, size, width), jnp.int32) for _, _, size in later],
        in_specs=[vmem, vmem, vmem, pl.BlockSpec(memory_space=pltpu.SMEM), hbm, hbm],
        out_specs=[vmem] * (count + 2 + len(later)),
        scratch_shapes=[
            pltpu.VMEM((count, depth, ROWS, width), jnp.float32),
            pltpu.VMEM((count, depth, ROWS, width), jnp.float32),
            pltpu.VMEM((count - 1, depth, early, width), jnp.int32),
            pltpu.SemaphoreType.DMA((count, 3)),
            pltpu.SemaphoreType.DMA((len(later),)),
        ],
        compiler_params=params,
        cost_estimate=cost(depth * height * width),
        name="pack",
    )(above, below, table, march_order, in_hbm(field), in_hbm(bins))
    messages = {}
    for slot in partners:
        messages[slot] = send("message", packed[slot - 1], slot)
    edges, entries, flips = packed[count - 1 : count + 2]
    cuts = packed[count + 2 :]

    slab = pl.pallas_call(
        functools.partial(side_kernel, count, depth),
        out_shape=pltpu.VMEM((total, rows, LANES), jnp.float32),
        in_specs=[hbm] + [vmem] * (count - 1),
        out_specs=vmem,
        scratch_shapes=[pltpu.VMEM((depth, rows, LANES), jnp.float32), pltpu.SemaphoreType.DMA],
        compiler_params=params,
        cost_estimate=cost(total * rows * LANES),
        name="side",
    )(in_hbm(field), *[bricks[slot] for slot in slots[1:]])
    beside = partner(slab, "sx", 1)

    ext, scaled, inner, known, token = pl.pallas_call(
        functools.partial(inner_kernel, count, depth),
        out_shape=(
            pltpu.VMEM((total + 2, rows + 2 * ROWS, width + 2 * LANES), jnp.float32),
            pltpu.VMEM((total, rows, width), jnp.float32),
            pltpu.VMEM((total, max(rows - 2 * ROWS, ROWS), width), jnp.float32),
            pltpu.VMEM((2, depth, rows, width), jnp.int32),
            jax.ShapeDtypeStruct((ROWS, LANES), jnp.float32),
        ),
        in_specs=[hbm] + [vmem] * (count + 3),
        out_specs=[vmem] * 5,
        scratch_shapes=[pltpu.VMEM((depth, rows, width), jnp.float32), pltpu.SemaphoreType.DMA],
        compiler_params=params,
        cost_estimate=cost(total * rows * width),
        name="inner",
    )(in_hbm(field), edges, beside, entries, *[bricks[slot] for slot in slots[1:]], cuts[0])
    done["inner"] = token

    image_shape = jax.ShapeDtypeStruct((4, rows, width), jnp.float32)
    outer, image = pl.pallas_call(
        functools.partial(outer_kernel, count, depth),
        out_shape=(pltpu.VMEM((total, 2 * ROWS, width), jnp.float32), image_shape),
        in_specs=[vmem] * (count + 5),
        out_specs=(vmem, hbm),
        scratch_shapes=[
            pltpu.VMEM((4, early, width), jnp.float32),
            pltpu.SemaphoreType.DMA((early // ROWS, COPIES)),
        ],
        compiler_params=params,
        cost_estimate=cost(total * rows * width),
        name="outer",
    )(entries, flips, ext, scaled, inner, known, *[messages[slot] for slot in slots[1:]])
    if not late:
        return image

    arrived = [send("bins", cut, slot) for (slot, _, _), cut in zip(later[1:], cuts[1:])]
    found = pl.pallas_call(
        functools.partial(look_kernel, depth),
        out_shape=pltpu.VMEM((2, depth, late, width), jnp.int32),
        in_specs=[vmem] * 2,
        out_specs=vmem,
        compiler_params=params,
        cost_estimate=cost(depth * late * width),
        name="look",
    )(entries, arrived[0])
    for index, (top, size) in enumerate(pieces):
        labels = arrived[1 + index * len(others) : 1 + (index + 1) * len(others)]
        labels = [labels[others.index(slot)] for slot in sorted(others)]
        shading = outer if top + size == rows else inner
        operands = [entries, flips, scaled, shading, known, found, *labels, image]
        image = pl.pallas_call(
            functools.partial(blend_kernel, count, depth, top, early, lead),
            out_shape=image_shape,
            in_specs=[vmem] * (len(operands) - 1) + [hbm],
            out_specs=hbm,
            scratch_shapes=[
                pltpu.VMEM((4, size, width), jnp.float32),
                pltpu.SemaphoreType.DMA((size // ROWS, COPIES)),
            ],
            input_output_aliases={len(operands) - 1: 0},
            compiler_params=params,
            cost_estimate=cost(total * size * width),
            name="blend",
        )(*operands)
    return image


def solution(mesh):
    placed = (P("gz", "sy", "sx"), P("gz", "sy", "sx"), P(), P("sy"))
    return jax.shard_map(
        shards, mesh=mesh, in_specs=placed, out_specs=P(None, ("sy", "gz"), "sx"), check_vma=False
    )
```

```python
import functools

import jax
import jax.numpy as jnp
from jax import lax
from jax.experimental import pallas as pl
from jax.experimental.pallas import tpu as pltpu
from jax.sharding import PartitionSpec as P

light_x = 0.36
light_y = 0.48
light_z = 0.8
LANES = 128
ROWS = 8
COLOUR_UNIT = 2.0**-12
OPACITY_UNIT = 2.0**-13
HALF_WORD = 16
LOG2_E = 1.4426950408889634
UNROLLED = 32
COPIES = 4
VMEM_LIMIT = 40 * 1024 * 1024

vmem = pl.BlockSpec(memory_space=pltpu.VMEM)
hbm = pl.BlockSpec(memory_space=pltpu.HBM)


def partner(x, axis, distance):
    return lax.ppermute(x, axis, [(i, i ^ distance) for i in range(lax.axis_size(axis))])


def in_hbm(array):
    return pltpu.with_memory_space_constraint(array, pltpu.HBM)


def after(array, *others):
    return lax.optimization_barrier((array, *others))[0]


def run_copies(moves):
    for move in moves:
        move.start()
    for move in moves:
        move.wait()


def lead_kernel(count, slot, field, piece, sem):
    rows = piece.shape[1]
    start = pl.multiple_of((lax.axis_index("gz") ^ slot) * rows, ROWS)
    run_copies([pltpu.make_async_copy(field.at[:, pl.ds(start, rows)], piece, sem)])


def split_kernel(count, depth, slots, field, *refs):
    pieces = refs[: len(slots)]
    last, first, ends, sems = refs[len(slots) :]
    height = field.shape[1]
    rows = height // count
    rank = lax.axis_index("gz")
    moves = [
        pltpu.make_async_copy(field.at[:, height - ROWS :], ends.at[0], sems.at[0]),
        pltpu.make_async_copy(field.at[:, :ROWS], ends.at[1], sems.at[1]),
    ]
    for index, slot in enumerate(slots):
        start = pl.multiple_of((rank ^ slot) * rows, ROWS)
        moves.append(pltpu.make_async_copy(field.at[:, pl.ds(start, rows)], pieces[index], sems.at[2 + index]))
    run_copies(moves)
    for j in range(depth):
        last[j : j + 1, :] = ends[0, j, ROWS - 1 :, :]
        first[j : j + 1, :] = ends[1, j, :1, :]


def pack_kernel(count, depth, early, later, above, below, table, march, field, bins, *refs):
    messages = refs[: count - 1]
    edges, entries, flips, *pieces, high, low, labels, sems, cut_sems = refs[count - 1 :]
    height, width = field.shape[1:]
    rows = height // count
    half = width // 2
    rank = lax.axis_index("gz")
    copies = []
    for slot in range(count):
        target = rank ^ slot
        top = pl.multiple_of(jnp.maximum(target * rows - ROWS, 0), ROWS)
        bottom = pl.multiple_of(jnp.minimum(target * rows + rows, height - ROWS), ROWS)
        start = pl.multiple_of(target * rows, ROWS)
        moves = [
            pltpu.make_async_copy(field.at[:, pl.ds(top, ROWS)], high.at[slot], sems.at[slot, 0]),
            pltpu.make_async_copy(field.at[:, pl.ds(bottom, ROWS)], low.at[slot], sems.at[slot, 1]),
        ]
        if slot:
            moves.append(
                pltpu.make_async_copy(bins.at[:, pl.ds(start, early)], labels.at[slot - 1], sems.at[slot, 2])
            )
        for move in moves:
            move.start()
        copies.append(moves)
    cuts = []
    for index, (slot, top, size) in enumerate(later):
        start = pl.multiple_of((rank ^ slot) * rows + top, ROWS)
        cuts.append(pltpu.make_async_copy(bins.at[:, pl.ds(start, size)], pieces[index], cut_sems.at[index]))
        cuts[-1].start()
    pair = pack_entries(table)
    for word in range(2):
        entries[word] = pair[word]
    for row in range(rows):
        flips[row : row + 1, :] = jnp.full((1, LANES), march[rank * rows + row], jnp.int32)
    for slot in range(count):
        target = rank ^ slot
        for move in copies[slot]:
            move.wait()
        message = messages[slot - 1] if slot else edges
        for j in range(depth):
            upper = jnp.where(target == 0, above[j : j + 1, :], high[slot, j, ROWS - 1 : ROWS, :])
            lower = jnp.where(target == count - 1, below[j : j + 1, :], low[slot, j, 0:1, :])
            for h in range(2):
                cols = slice(h * half, (h + 1) * half)
                at = 2 * depth * h + j
                message[at : at + 1, :] = upper[:, cols]
                message[at + depth : at + depth + 1, :] = lower[:, cols]
                if slot:
                    first = 4 * depth + (2 * j + h) * early
                    message[first : first + early, :] = labels[slot - 1, j, :, cols].astype(jnp.float32)
    for move in cuts:
        move.wait()


def side_kernel(count, depth, field, *refs):
    bricks = (None,) + refs[: count - 1]
    slab, own, sem = refs[count - 1 :]
    rows = slab.shape[1]
    width = field.shape[2]
    side = lax.axis_index("sx")
    start = pl.multiple_of(lax.axis_index("gz") * rows, ROWS)
    column = pl.multiple_of((1 - side) * (width - LANES), LANES)
    move = pltpu.make_async_copy(field.at[:, pl.ds(start, rows), pl.ds(column, LANES)], own, sem)
    move.start()
    for slot in range(1, count):
        for j in range(depth):
            slab[slot * depth + j] = jnp.where(
                side == 1, bricks[slot][j, :, :LANES], bricks[slot][j, :, width - LANES :]
            )
    move.wait()
    for j in range(depth):
        slab[j] = own[j]


def pack_entries(table):
    units = [1.0 / COLOUR_UNIT] * 3 + [1.0 / OPACITY_UNIT]
    rows = [
        jnp.broadcast_to((table[c : c + 1, :] * units[c]).astype(jnp.int32), (ROWS, table.shape[1])) for c in range(4)
    ]
    return rows[0] | rows[1] << HALF_WORD, rows[2] | rows[3] << HALF_WORD


def look(entries, labels):
    return jnp.take_along_axis(entries, labels, axis=1, mode="promise_in_bounds")


def low_part(words):
    return (words & ((1 << HALF_WORD) - 1)).astype(jnp.float32)


def high_part(words):
    return (words >> HALF_WORD).astype(jnp.float32)


def blend_rows(count, depth, words, back, scaled, span, shading, shaded, result, here, finish):
    rank = lax.axis_index("gz")
    tiles = result.shape[2] // LANES
    unroll = max(min(tiles // COPIES, UNROLLED // (count * depth)), 1)
    ahead = [
        [jnp.where((rank ^ other) < (rank ^ slot), 1.0, 0.0) for other in range(count)] for slot in range(count)
    ]

    def blend_tile(cols, h):
        found = [words(cell, cols, h) for cell in range(count * depth)]
        taus = [high_part(found[cell][1]) * scaled[cell, span, cols] for cell in range(count * depth)]
        inner = []
        for slot in range(count):
            sums = [taus[slot * depth]]
            for j in range(1, depth):
                sums.append(sums[-1] + taus[slot * depth + j])
            inner.append(sums)
        whole = sum(sums[-1] for sums in inner)
        sign = jnp.where(back, 1.0, -1.0)
        shift = jnp.where(back, -whole, 0.0)
        colour = [jnp.zeros((ROWS, LANES), jnp.float32) for _ in range(3)]
        for slot in range(count):
            front = sum(inner[other][-1] * ahead[slot][other] for other in range(count) if other != slot)
            reached = [front] + [front + part for part in inner[slot]]
            through = [jnp.exp2(sign * part + shift) for part in reached]
            for j in range(depth):
                cell = slot * depth + j
                weight = jnp.abs(through[j] - through[j + 1]) * shading[cell, shaded, cols]
                colour[0] = colour[0] + weight * low_part(found[cell][0])
                colour[1] = colour[1] + weight * high_part(found[cell][0])
                colour[2] = colour[2] + weight * low_part(found[cell][1])
        for c in range(3):
            result[c, here, cols] = colour[c]
        result[3, here, cols] = 1.0 - jnp.exp2(-whole)

    quarter = tiles // COPIES
    for part in range(COPIES):
        h = 2 * part // COPIES
        if unroll == quarter:
            for tile in range(part * quarter, (part + 1) * quarter):
                blend_tile(slice(tile * LANES, (tile + 1) * LANES), h)
        else:

            def tile_step(step, _, part=part, h=h):
                for tile in range(unroll):
                    left = (part * quarter + step * unroll + tile) * LANES
                    blend_tile(pl.ds(pl.multiple_of(left, LANES), LANES), h)
                return 0

            lax.fori_loop(0, quarter // unroll, tile_step, 0)
        finish(part)


def copy_out(result, image, sems, top, start):
    columns = result.shape[2] // COPIES
    return [
        pltpu.make_async_copy(
            result.at[:, top : top + ROWS, part * columns : (part + 1) * columns],
            image.at[:, start + top : start + top + ROWS, part * columns : (part + 1) * columns],
            sems.at[top // ROWS, part],
        )
        for part in range(COPIES)
    ]


def shade_tile(ext, at, top, width, dy_of, store):
    here = slice(ROWS + top, 2 * ROWS + top)
    lane = lax.broadcasted_iota(jnp.int32, (ROWS, LANES), 1)
    first = lane == 0
    last = lane == LANES - 1
    tiles = [ext[at + 1, here, left : left + LANES] for left in range(0, width + 2 * LANES, LANES)]
    toward = [pltpu.roll(tile, LANES - 1, 1) for tile in tiles]
    away = [pltpu.roll(tile, 1, 1) for tile in tiles]
    for c in range(1, width // LANES + 1):
        cols = slice(c * LANES, (c + 1) * LANES)
        dx = jnp.where(last, toward[c + 1], toward[c]) - jnp.where(first, away[c - 1], away[c])
        dy = dy_of(
            c - 1,
            ext[at + 1, ROWS + top + 1 : 2 * ROWS + top + 1, cols]
            - ext[at + 1, ROWS + top - 1 : 2 * ROWS + top - 1, cols],
        )
        dz = ext[at + 2, here, cols] - ext[at, here, cols]
        facing = jnp.abs((0.5 * light_x) * dx + (0.5 * light_y) * dy + (0.5 * light_z) * dz)
        square = 0.25 * (dx * dx + dy * dy + dz * dz) + 1.0
        store(c - 1, 0.3 * COLOUR_UNIT + (0.7 * COLOUR_UNIT) * facing * lax.rsqrt(square))


def inner_kernel(count, depth, field, edges, beside, entries, *refs):
    parts = len(refs) - (count - 1) - 7
    bricks = refs[: count - 1]
    own_bins = refs[count - 1 : count - 1 + parts]
    ext, scaled, inner, known, token, own_brick, sem = refs[count - 1 + parts :]
    rows, width = scaled.shape[1:]
    half = width // 2
    total = count * depth
    rank = lax.axis_index("gz")
    side = lax.axis_index("sx")
    inside = slice(ROWS, ROWS + rows)
    move = pltpu.make_async_copy(field.at[:, pl.ds(pl.multiple_of(rank * rows, ROWS), rows)], own_brick, sem)
    move.start()
    bricks = (own_brick, *bricks)
    zero_plane = jnp.zeros((rows, width), jnp.float32)
    zero_row = jnp.zeros((ROWS, width), jnp.float32)
    ext[0, inside, LANES : LANES + width] = zero_plane
    ext[total + 1, inside, LANES : LANES + width] = zero_plane
    for slot in reversed(range(count)):
        if slot == 0:
            move.wait()
        for j in range(depth):
            at = (rank ^ slot) * depth + j
            plane = bricks[slot][j]
            scaled[slot * depth + j] = plane * (OPACITY_UNIT * LOG2_E)
            ext[at + 1, inside, LANES : LANES + width] = plane
            ext[at + 1, :ROWS, LANES : LANES + width] = zero_row
            ext[at + 1, ROWS + rows :, LANES : LANES + width] = zero_row
            if slot == 0:
                for h in range(2):
                    cols = slice(LANES + h * half, LANES + (h + 1) * half)
                    row = 2 * depth * h + j
                    ext[at + 1, ROWS - 1 : ROWS, cols] = edges[row : row + 1, :]
                    ext[at + 1, ROWS + rows : ROWS + rows + 1, cols] = edges[row + depth : row + depth + 1, :]
            column = beside[slot * depth + j]
            ext[at + 1, inside, :LANES] = jnp.where(side == 1, column, 0.0)
            ext[at + 1, inside, LANES + width :] = jnp.where(side == 0, column, 0.0)
    pair = (entries[0], entries[1])
    start = 0
    for part in own_bins:
        size = part.shape[1]
        for j in range(depth):
            for top in range(0, size, ROWS):
                for left in range(0, width, LANES):
                    cols = slice(left, left + LANES)
                    labels = part[j, top : top + ROWS, cols]
                    for word in range(2):
                        known[word, j, start + top : start + top + ROWS, cols] = look(pair[word], labels)
        start += size

    def plane_step(cell, _):
        at = (rank ^ (cell // depth)) * depth + cell % depth
        for top in range(ROWS, rows - ROWS, ROWS):

            def store(c, value, top=top):
                inner[cell, top - ROWS : top, c * LANES : (c + 1) * LANES] = value

            shade_tile(ext, at, top, width, lambda c, dy: dy, store)
        return 0

    if rows > 2 * ROWS:
        lax.fori_loop(0, total, plane_step, 0)
    else:
        inner[...] = jnp.zeros_like(inner)
    token[...] = jnp.zeros_like(token)


def outer_kernel(count, depth, entries, flips, ext, scaled, inner, known, *refs):
    messages = refs[: count - 1]
    outer, image, result, sems = refs[count - 1 :]
    rows, width = scaled.shape[1:]
    early = result.shape[1]
    half = width // 2
    rank = lax.axis_index("gz")
    pair = (entries[0], entries[1])
    row_of = lax.broadcasted_iota(jnp.int32, (ROWS, LANES), 0)

    def shade(top):
        for cell in range(count * depth):
            slot, j = divmod(cell, depth)
            at = (rank ^ slot) * depth + j

            def dy_of(c, dy, slot=slot, j=j):
                if slot == 0:
                    return dy
                h, left = c * LANES // half, c * LANES % half
                row = 2 * depth * h + j
                cols = slice(left, left + LANES)
                if top == 0:
                    dy = dy - jnp.where(row_of == 0, messages[slot - 1][row : row + 1, cols], 0.0)
                if top == rows - ROWS:
                    beyond = messages[slot - 1][row + depth : row + depth + 1, cols]
                    dy = dy + jnp.where(row_of == ROWS - 1, beyond, 0.0)
                return dy

            def store(c, value, cell=cell):
                place = 0 if top == 0 else ROWS
                outer[cell, place : place + ROWS, c * LANES : (c + 1) * LANES] = value

            shade_tile(ext, at, top, width, dy_of, store)

    shade(0)
    copies = []
    for top in range(0, early, ROWS):
        here = slice(top, top + ROWS)

        def words(cell, cols, h, top=top):
            slot, j = divmod(cell, depth)
            if slot == 0:
                return tuple(known[word, j, top : top + ROWS, cols] for word in range(2))
            left = cols.start - h * half
            left = pl.ds(left if isinstance(left, int) else pl.multiple_of(left, LANES), LANES)
            row = 4 * depth + (2 * j + h) * early + top
            labels = messages[slot - 1][row : row + ROWS, left].astype(jnp.int32)
            return look(pair[0], labels), look(pair[1], labels)

        parts = copy_out(result, image, sems, top, 0)
        shading, shaded = (outer, slice(0, ROWS)) if top == 0 else (inner, slice(top - ROWS, top))
        blend_rows(
            count, depth, words, flips[here, :] == 1, scaled, here, shading, shaded, result, here,
            lambda part, parts=parts: parts[part].start(),
        )
        copies += parts
    if rows > ROWS:
        shade(rows - ROWS)
    for move in copies:
        move.wait()


def look_kernel(depth, entries, brick, found):
    rows, width = found.shape[2:]
    for j in range(depth):
        for top in range(0, rows, ROWS):
            for left in range(0, width, LANES):
                at = (slice(top, top + ROWS), slice(left, left + LANES))
                labels = brick[(j, *at)]
                for word in range(2):
                    found[(word, j, *at)] = look(entries[word], labels)


def blend_kernel(count, depth, start, late, lead, entries, flips, scaled, shading, known, found, *refs):
    bricks = refs[: count - 2]
    image, result, sems = refs[-3:]
    rows = result.shape[1]
    pair = (entries[0], entries[1])
    unknown = [slot for slot in range(1, count) if slot != lead]
    copies = []
    for top in range(0, rows, ROWS):
        here = slice(top, top + ROWS)
        span = slice(start + top, start + top + ROWS)
        inner = start + top + ROWS < scaled.shape[1]
        shaded = slice(start + top - ROWS, start + top) if inner else slice(ROWS, 2 * ROWS)

        def words(cell, cols, h, here=here, span=span, top=top):
            slot, j = divmod(cell, depth)
            if slot == 0:
                return tuple(known[word, j, span, cols] for word in range(2))
            if slot == lead:
                begin = start + top - late
                return tuple(found[word, j, begin : begin + ROWS, cols] for word in range(2))
            labels = bricks[unknown.index(slot)][j, here, cols]
            return look(pair[0], labels), look(pair[1], labels)

        parts = copy_out(result, image, sems, top, start)
        blend_rows(
            count, depth, words, flips[span, :] == 1, scaled, span, shading, shaded, result, here,
            lambda part, parts=parts: parts[part].start(),
        )
        copies += parts
    for move in copies:
        move.wait()


def shards(field, bins, table, march_order):
    depth, height, width = field.shape
    count = lax.axis_size("gz")
    rank = lax.axis_index("gz").astype(jnp.int32)
    rows = height // count
    total = count * depth
    half = width // 2
    slots = range(count)
    partners = sorted(range(1, count), key=lambda slot: (-slot.bit_count(), slot))
    lead, *others = partners
    params = pltpu.CompilerParams(vmem_limit_bytes=VMEM_LIMIT)

    def cost(cells):
        return pl.CostEstimate(flops=20 * cells, bytes_accessed=8 * cells, transcendentals=cells)

    done = {}
    order = {"message": lambda index: [("field", 0)], "bins": lambda index: [("message", index), "inner"]}

    def send(name, array, slot):
        index = partners.index(slot)
        waits = [done[key] for key in order.get(name, lambda index: ())(index)]
        done[name, index] = partner(after(array, *waits), "gz", slot)
        return done[name, index]

    bricks = {}
    sent = pl.pallas_call(
        functools.partial(lead_kernel, count, lead),
        out_shape=pltpu.VMEM((depth, rows, width), jnp.float32),
        in_specs=[hbm],
        out_specs=vmem,
        scratch_shapes=[pltpu.SemaphoreType.DMA],
        compiler_params=params,
        cost_estimate=cost(depth * rows * width),
        name="lead",
    )(in_hbm(field))
    bricks[lead] = send("field", sent, lead)

    *pieces, last, first = pl.pallas_call(
        functools.partial(split_kernel, count, depth, others),
        out_shape=[pltpu.VMEM((depth, rows, width), jnp.float32)] * len(others)
        + [pltpu.VMEM((depth, width), jnp.float32)] * 2,
        in_specs=[hbm],
        out_specs=[vmem] * count,
        scratch_shapes=[pltpu.VMEM((2, depth, ROWS, width), jnp.float32), pltpu.SemaphoreType.DMA((count,))],
        compiler_params=params,
        cost_estimate=cost(depth * height * width),
        name="split",
    )(in_hbm(after(field, sent)))
    for slot, sent in zip(others, pieces):
        bricks[slot] = send("field", sent, slot)

    forward = [(i, i + 1) for i in range(lax.axis_size("sy") - 1)]
    backward = [(target, origin) for origin, target in forward]
    above = lax.ppermute(last, "sy", forward)
    below = lax.ppermute(first, "sy", backward)

    early = max(rows // 2 // ROWS, 1) * ROWS
    late = rows - early
    later = []
    if late:
        later = [(0, 0, rows), (lead, early, late)]
        pieces = [(early, late - ROWS), (rows - ROWS, ROWS)] if late > ROWS else [(early, late)]
        later += [(slot, top, size) for top, size in pieces for slot in others]
    else:
        pieces = []
        later = [(0, 0, rows)]
    message_rows = 4 * depth + 2 * depth * early
    packed = pl.pallas_call(
        functools.partial(pack_kernel, count, depth, early, later),
        out_shape=[pltpu.VMEM((message_rows, half), jnp.float32)] * (count - 1)
        + [
            jax.ShapeDtypeStruct((4 * depth, half), jnp.float32),
            jax.ShapeDtypeStruct((2, ROWS, table.shape[1]), jnp.int32),
            jax.ShapeDtypeStruct((rows, LANES), jnp.int32),
        ]
        + [jax.ShapeDtypeStruct((depth, size, width), jnp.int32) for _, _, size in later],
        in_specs=[vmem, vmem, vmem, pl.BlockSpec(memory_space=pltpu.SMEM), hbm, hbm],
        out_specs=[vmem] * (count + 2 + len(later)),
        scratch_shapes=[
            pltpu.VMEM((count, depth, ROWS, width), jnp.float32),
            pltpu.VMEM((count, depth, ROWS, width), jnp.float32),
            pltpu.VMEM((count - 1, depth, early, width), jnp.int32),
            pltpu.SemaphoreType.DMA((count, 3)),
            pltpu.SemaphoreType.DMA((len(later),)),
        ],
        compiler_params=params,
        cost_estimate=cost(depth * height * width),
        name="pack",
    )(above, below, table.astype(jnp.float32), march_order, in_hbm(field), in_hbm(bins))
    messages = {}
    for slot in partners:
        messages[slot] = send("message", packed[slot - 1], slot)
    edges, entries, flips = packed[count - 1 : count + 2]
    cuts = packed[count + 2 :]

    slab = pl.pallas_call(
        functools.partial(side_kernel, count, depth),
        out_shape=pltpu.VMEM((total, rows, LANES), jnp.float32),
        in_specs=[hbm] + [vmem] * (count - 1),
        out_specs=vmem,
        scratch_shapes=[pltpu.VMEM((depth, rows, LANES), jnp.float32), pltpu.SemaphoreType.DMA],
        compiler_params=params,
        cost_estimate=cost(total * rows * LANES),
        name="side",
    )(in_hbm(field), *[bricks[slot] for slot in slots[1:]])
    beside = partner(slab, "sx", 1)

    ext, scaled, inner, known, token = pl.pallas_call(
        functools.partial(inner_kernel, count, depth),
        out_shape=(
            pltpu.VMEM((total + 2, rows + 2 * ROWS, width + 2 * LANES), jnp.float32),
            pltpu.VMEM((total, rows, width), jnp.float32),
            pltpu.VMEM((total, max(rows - 2 * ROWS, ROWS), width), jnp.float32),
            pltpu.VMEM((2, depth, rows, width), jnp.int32),
            jax.ShapeDtypeStruct((ROWS, LANES), jnp.float32),
        ),
        in_specs=[hbm] + [vmem] * (count + 3),
        out_specs=[vmem] * 5,
        scratch_shapes=[pltpu.VMEM((depth, rows, width), jnp.float32), pltpu.SemaphoreType.DMA],
        compiler_params=params,
        cost_estimate=cost(total * rows * width),
        name="inner",
    )(in_hbm(field), edges, beside, entries, *[bricks[slot] for slot in slots[1:]], cuts[0])
    done["inner"] = token

    image_shape = jax.ShapeDtypeStruct((4, rows, width), jnp.float32)
    outer, image = pl.pallas_call(
        functools.partial(outer_kernel, count, depth),
        out_shape=(pltpu.VMEM((total, 2 * ROWS, width), jnp.float32), image_shape),
        in_specs=[vmem] * (count + 5),
        out_specs=(vmem, hbm),
        scratch_shapes=[
            pltpu.VMEM((4, early, width), jnp.float32),
            pltpu.SemaphoreType.DMA((early // ROWS, COPIES)),
        ],
        compiler_params=params,
        cost_estimate=cost(total * rows * width),
        name="outer",
    )(entries, flips, ext, scaled, inner, known, *[messages[slot] for slot in slots[1:]])
    if not late:
        return image

    arrived = [send("bins", cut, slot) for (slot, _, _), cut in zip(later[1:], cuts[1:])]
    found = pl.pallas_call(
        functools.partial(look_kernel, depth),
        out_shape=pltpu.VMEM((2, depth, late, width), jnp.int32),
        in_specs=[vmem] * 2,
        out_specs=vmem,
        compiler_params=params,
        cost_estimate=cost(depth * late * width),
        name="look",
    )(entries, arrived[0])
    for index, (top, size) in enumerate(pieces):
        labels = arrived[1 + index * len(others) : 1 + (index + 1) * len(others)]
        labels = [labels[others.index(slot)] for slot in sorted(others)]
        shading = outer if top + size == rows else inner
        operands = [entries, flips, scaled, shading, known, found, *labels, image]
        image = pl.pallas_call(
            functools.partial(blend_kernel, count, depth, top, early, lead),
            out_shape=image_shape,
            in_specs=[vmem] * (len(operands) - 1) + [hbm],
            out_specs=hbm,
            scratch_shapes=[
                pltpu.VMEM((4, size, width), jnp.float32),
                pltpu.SemaphoreType.DMA((size // ROWS, COPIES)),
            ],
            input_output_aliases={len(operands) - 1: 0},
            compiler_params=params,
            cost_estimate=cost(total * size * width),
            name="blend",
        )(*operands)
    return image


def solution(mesh):
    placed = (P("gz", "sy", "sx"), P("gz", "sy", "sx"), P(), P("sy"))
    return jax.shard_map(
        shards, mesh=mesh, in_specs=placed, out_specs=P(None, ("sy", "gz"), "sx"), check_vma=False
    )
```

```python
import functools

import jax
import jax.numpy as jnp
from jax import lax
from jax.experimental import pallas as pl
from jax.experimental.pallas import tpu as pltpu
from jax.sharding import PartitionSpec as P

light_x = 0.36
light_y = 0.48
light_z = 0.8
LANES = 128
ROWS = 8
COLOUR_UNIT = 2.0**-12
OPACITY_UNIT = 2.0**-13
HALF_WORD = 16
LOG2_E = 1.4426950408889634
UNROLLED = 32
COPIES = 4
VMEM_LIMIT = 40 * 1024 * 1024

vmem = pl.BlockSpec(memory_space=pltpu.VMEM)
hbm = pl.BlockSpec(memory_space=pltpu.HBM)


def partner(x, axis, distance):
    return lax.ppermute(x, axis, [(i, i ^ distance) for i in range(lax.axis_size(axis))])


def in_hbm(array):
    return pltpu.with_memory_space_constraint(array, pltpu.HBM)


def after(array, *others):
    return lax.optimization_barrier((array, *others))[0]


def run_copies(moves):
    for move in moves:
        move.start()
    for move in moves:
        move.wait()


def lead_kernel(count, slot, field, piece, sem):
    rows = piece.shape[1]
    start = pl.multiple_of((lax.axis_index("gz") ^ slot) * rows, ROWS)
    run_copies([pltpu.make_async_copy(field.at[:, pl.ds(start, rows)], piece, sem)])


def split_kernel(count, depth, slots, field, *refs):
    pieces = refs[: len(slots)]
    last, first, ends, sems = refs[len(slots) :]
    height = field.shape[1]
    rows = height // count
    rank = lax.axis_index("gz")
    moves = [
        pltpu.make_async_copy(field.at[:, height - ROWS :], ends.at[0], sems.at[0]),
        pltpu.make_async_copy(field.at[:, :ROWS], ends.at[1], sems.at[1]),
    ]
    for index, slot in enumerate(slots):
        start = pl.multiple_of((rank ^ slot) * rows, ROWS)
        moves.append(pltpu.make_async_copy(field.at[:, pl.ds(start, rows)], pieces[index], sems.at[2 + index]))
    run_copies(moves)
    for j in range(depth):
        last[j : j + 1, :] = ends[0, j, ROWS - 1 :, :]
        first[j : j + 1, :] = ends[1, j, :1, :]


def pack_kernel(count, depth, early, later, above, below, table, march, field, bins, *refs):
    messages = refs[: count - 1]
    edges, entries, flips, *pieces, high, low, labels, sems, cut_sems = refs[count - 1 :]
    height, width = field.shape[1:]
    rows = height // count
    half = width // 2
    rank = lax.axis_index("gz")
    copies = []
    for slot in range(count):
        target = rank ^ slot
        top = pl.multiple_of(jnp.maximum(target * rows - ROWS, 0), ROWS)
        bottom = pl.multiple_of(jnp.minimum(target * rows + rows, height - ROWS), ROWS)
        start = pl.multiple_of(target * rows, ROWS)
        moves = [
            pltpu.make_async_copy(field.at[:, pl.ds(top, ROWS)], high.at[slot], sems.at[slot, 0]),
            pltpu.make_async_copy(field.at[:, pl.ds(bottom, ROWS)], low.at[slot], sems.at[slot, 1]),
        ]
        if slot:
            moves.append(
                pltpu.make_async_copy(bins.at[:, pl.ds(start, early)], labels.at[slot - 1], sems.at[slot, 2])
            )
        for move in moves:
            move.start()
        copies.append(moves)
    cuts = []
    for index, (slot, top, size) in enumerate(later):
        start = pl.multiple_of((rank ^ slot) * rows + top, ROWS)
        cuts.append(pltpu.make_async_copy(bins.at[:, pl.ds(start, size)], pieces[index], cut_sems.at[index]))
        cuts[-1].start()
    pair = pack_entries(table)
    for word in range(2):
        entries[word] = pair[word]
    for row in range(rows):
        flips[row : row + 1, :] = jnp.full((1, LANES), march[rank * rows + row], jnp.int32)
    for slot in range(count):
        target = rank ^ slot
        for move in copies[slot]:
            move.wait()
        message = messages[slot - 1] if slot else edges
        for j in range(depth):
            upper = jnp.where(target == 0, above[j : j + 1, :], high[slot, j, ROWS - 1 : ROWS, :])
            lower = jnp.where(target == count - 1, below[j : j + 1, :], low[slot, j, 0:1, :])
            for h in range(2):
                cols = slice(h * half, (h + 1) * half)
                at = 2 * depth * h + j
                message[at : at + 1, :] = upper[:, cols]
                message[at + depth : at + depth + 1, :] = lower[:, cols]
                if slot:
                    first = 4 * depth + (2 * j + h) * early
                    message[first : first + early, :] = labels[slot - 1, j, :, cols].astype(jnp.float32)
    for move in cuts:
        move.wait()


def side_kernel(count, depth, field, *refs):
    bricks = (None,) + refs[: count - 1]
    slab, own, sem = refs[count - 1 :]
    rows = slab.shape[1]
    width = field.shape[2]
    side = lax.axis_index("sx")
    start = pl.multiple_of(lax.axis_index("gz") * rows, ROWS)
    column = pl.multiple_of((1 - side) * (width - LANES), LANES)
    move = pltpu.make_async_copy(field.at[:, pl.ds(start, rows), pl.ds(column, LANES)], own, sem)
    move.start()
    for slot in range(1, count):
        for j in range(depth):
            slab[slot * depth + j] = jnp.where(
                side == 1, bricks[slot][j, :, :LANES], bricks[slot][j, :, width - LANES :]
            )
    move.wait()
    for j in range(depth):
        slab[j] = own[j]


def pack_entries(table):
    units = [1.0 / COLOUR_UNIT] * 3 + [1.0 / OPACITY_UNIT]
    rows = [
        jnp.broadcast_to((table[c : c + 1, :] * units[c]).astype(jnp.int32), (ROWS, table.shape[1])) for c in range(4)
    ]
    return rows[0] | rows[1] << HALF_WORD, rows[2] | rows[3] << HALF_WORD


def look(entries, labels):
    return jnp.take_along_axis(entries, labels, axis=1, mode="promise_in_bounds")


def low_part(words):
    return (words & ((1 << HALF_WORD) - 1)).astype(jnp.float32)


def high_part(words):
    return (words >> HALF_WORD).astype(jnp.float32)


def in_front(sums, bit):
    if len(sums) == 1:
        return [None], sums[0]
    middle = len(sums) // 2
    low, low_sum = in_front(sums[:middle], bit - 1)
    high, high_sum = in_front(sums[middle:], bit - 1)
    swapped = jnp.where(lax.axis_index("gz") >> bit & 1 == 1, 1.0, 0.0)
    low_adds = high_sum * swapped
    high_adds = low_sum * (1.0 - swapped)
    fronts = [low_adds if front is None else front + low_adds for front in low]
    fronts += [high_adds if front is None else front + high_adds for front in high]
    return fronts, low_sum + high_sum


def cell_values(words, scaled, shade):
    return high_part(words[1]) * scaled, shade, (low_part(words[0]), high_part(words[0]), low_part(words[1]))


def blend_rows(count, depth, values, back, result, here, finish):
    tiles = result.shape[2] // LANES
    unroll = max(min(tiles // COPIES, UNROLLED // (count * depth)), 1)

    def blend_tile(cols, h):
        cells = [values(cell, cols, h) for cell in range(count * depth)]
        inner = []
        for slot in range(count):
            sums = [cells[slot * depth][0]]
            for j in range(1, depth):
                sums.append(sums[-1] + cells[slot * depth + j][0])
            inner.append(sums)
        fronts, whole = in_front([sums[-1] for sums in inner], count.bit_length() - 2)
        shift = jnp.where(back, -whole, 0.0)
        colour = [jnp.zeros((ROWS, LANES), jnp.float32) for _ in range(3)]
        for slot in range(count):
            base = fronts[slot] + shift
            through = [jnp.exp2(base)] + [jnp.exp2(base + part) for part in inner[slot]]
            for j in range(depth):
                _, shade, colours = cells[slot * depth + j]
                weight = jnp.abs(through[j] - through[j + 1])
                if shade is not None:
                    weight = weight * shade
                colour = [total + weight * part for total, part in zip(colour, colours)]
        for c in range(3):
            result[c, here, cols] = colour[c]
        result[3, here, cols] = 1.0 - jnp.exp2(-jnp.abs(whole))

    quarter = tiles // COPIES
    for part in range(COPIES):
        h = 2 * part // COPIES
        if unroll == quarter:
            for tile in range(part * quarter, (part + 1) * quarter):
                blend_tile(slice(tile * LANES, (tile + 1) * LANES), h)
        else:

            def tile_step(step, _, part=part, h=h):
                for tile in range(unroll):
                    left = (part * quarter + step * unroll + tile) * LANES
                    blend_tile(pl.ds(pl.multiple_of(left, LANES), LANES), h)
                return 0

            lax.fori_loop(0, quarter // unroll, tile_step, 0)
        finish(part)


def copy_out(result, image, sems, top, start):
    columns = result.shape[2] // COPIES
    return [
        pltpu.make_async_copy(
            result.at[:, top : top + ROWS, part * columns : (part + 1) * columns],
            image.at[:, start + top : start + top + ROWS, part * columns : (part + 1) * columns],
            sems.at[top // ROWS, part],
        )
        for part in range(COPIES)
    ]


def shade_tile(ext, at, top, width, dy_of, store):
    here = slice(ROWS + top, 2 * ROWS + top)
    lane = lax.broadcasted_iota(jnp.int32, (ROWS, LANES), 1)
    first = lane == 0
    last = lane == LANES - 1
    tiles = [ext[at + 1, here, left : left + LANES] for left in range(0, width + 2 * LANES, LANES)]
    toward = [pltpu.roll(tile, LANES - 1, 1) for tile in tiles]
    away = [pltpu.roll(tile, 1, 1) for tile in tiles]
    for c in range(1, width // LANES + 1):
        cols = slice(c * LANES, (c + 1) * LANES)
        dx = jnp.where(last, toward[c + 1], toward[c]) - jnp.where(first, away[c - 1], away[c])
        dy = dy_of(
            c - 1,
            ext[at + 1, ROWS + top + 1 : 2 * ROWS + top + 1, cols]
            - ext[at + 1, ROWS + top - 1 : 2 * ROWS + top - 1, cols],
        )
        dz = ext[at + 2, here, cols] - ext[at, here, cols]
        facing = jnp.abs((0.5 * light_x) * dx + (0.5 * light_y) * dy + (0.5 * light_z) * dz)
        square = 0.25 * (dx * dx + dy * dy + dz * dz) + 1.0
        store(c - 1, 0.3 * COLOUR_UNIT + (0.7 * COLOUR_UNIT) * facing * lax.rsqrt(square))


def inner_kernel(count, depth, field, edges, beside, entries, flips, *refs):
    parts = len(refs) - (count - 1) - 7
    bricks = refs[: count - 1]
    own_bins = refs[count - 1 : count - 1 + parts]
    ext, scaled, inner, known, token, own_brick, sem = refs[count - 1 + parts :]
    rows, width = scaled.shape[1:]
    half = width // 2
    total = count * depth
    rank = lax.axis_index("gz")
    side = lax.axis_index("sx")
    inside = slice(ROWS, ROWS + rows)
    move = pltpu.make_async_copy(field.at[:, pl.ds(pl.multiple_of(rank * rows, ROWS), rows)], own_brick, sem)
    move.start()
    bricks = (own_brick, *bricks)
    unit = jnp.where(flips[...] == 1, OPACITY_UNIT * LOG2_E, -OPACITY_UNIT * LOG2_E)
    zero_plane = jnp.zeros((rows, width), jnp.float32)
    zero_row = jnp.zeros((ROWS, width), jnp.float32)
    ext[0, inside, LANES : LANES + width] = zero_plane
    ext[total + 1, inside, LANES : LANES + width] = zero_plane
    for slot in reversed(range(count)):
        if slot == 0:
            move.wait()
        for j in range(depth):
            at = (rank ^ slot) * depth + j
            plane = bricks[slot][j]
            for left in range(0, width, LANES):
                cols = slice(left, left + LANES)
                scaled[slot * depth + j, :, cols] = bricks[slot][j, :, cols] * unit
            ext[at + 1, inside, LANES : LANES + width] = plane
            ext[at + 1, :ROWS, LANES : LANES + width] = zero_row
            ext[at + 1, ROWS + rows :, LANES : LANES + width] = zero_row
            if slot == 0:
                for h in range(2):
                    cols = slice(LANES + h * half, LANES + (h + 1) * half)
                    row = 2 * depth * h + j
                    ext[at + 1, ROWS - 1 : ROWS, cols] = edges[row : row + 1, :]
                    ext[at + 1, ROWS + rows : ROWS + rows + 1, cols] = edges[row + depth : row + depth + 1, :]
            column = beside[slot * depth + j]
            ext[at + 1, inside, :LANES] = jnp.where(side == 1, column, 0.0)
            ext[at + 1, inside, LANES + width :] = jnp.where(side == 0, column, 0.0)
    pair = (entries[0], entries[1])
    start = 0
    for part in own_bins:
        size = part.shape[1]
        for j in range(depth):
            for top in range(0, size, ROWS):
                for left in range(0, width, LANES):
                    cols = slice(left, left + LANES)
                    labels = part[j, top : top + ROWS, cols]
                    for word in range(2):
                        known[word, j, start + top : start + top + ROWS, cols] = look(pair[word], labels)
        start += size

    def plane_step(cell, _):
        at = (rank ^ (cell // depth)) * depth + cell % depth
        for top in range(ROWS, rows - ROWS, ROWS):

            def store(c, value, top=top):
                inner[cell, top - ROWS : top, c * LANES : (c + 1) * LANES] = value

            shade_tile(ext, at, top, width, lambda c, dy: dy, store)
        return 0

    if rows > 2 * ROWS:
        lax.fori_loop(0, total, plane_step, 0)
    else:
        inner[...] = jnp.zeros_like(inner)
    token[...] = jnp.zeros_like(token)


def outer_kernel(count, depth, entries, flips, ext, scaled, inner, known, *refs):
    messages = refs[: count - 1]
    outer, image, result, sems = refs[count - 1 :]
    rows, width = scaled.shape[1:]
    early = result.shape[1]
    half = width // 2
    rank = lax.axis_index("gz")
    pair = (entries[0], entries[1])
    row_of = lax.broadcasted_iota(jnp.int32, (ROWS, LANES), 0)

    def shade(top):
        for cell in range(count * depth):
            slot, j = divmod(cell, depth)
            at = (rank ^ slot) * depth + j

            def dy_of(c, dy, slot=slot, j=j):
                if slot == 0:
                    return dy
                h, left = c * LANES // half, c * LANES % half
                row = 2 * depth * h + j
                cols = slice(left, left + LANES)
                if top == 0:
                    dy = dy - jnp.where(row_of == 0, messages[slot - 1][row : row + 1, cols], 0.0)
                if top == rows - ROWS:
                    beyond = messages[slot - 1][row + depth : row + depth + 1, cols]
                    dy = dy + jnp.where(row_of == ROWS - 1, beyond, 0.0)
                return dy

            def store(c, value, cell=cell):
                place = 0 if top == 0 else ROWS
                outer[cell, place : place + ROWS, c * LANES : (c + 1) * LANES] = value

            shade_tile(ext, at, top, width, dy_of, store)

    shade(0)
    copies = []
    for top in range(0, early, ROWS):
        here = slice(top, top + ROWS)

        shading, shaded = (outer, slice(0, ROWS)) if top == 0 else (inner, slice(top - ROWS, top))

        def values(cell, cols, h, top=top, shading=shading, shaded=shaded):
            slot, j = divmod(cell, depth)
            if slot == 0:
                words = tuple(known[word, j, top : top + ROWS, cols] for word in range(2))
            else:
                left = cols.start - h * half
                left = pl.ds(left if isinstance(left, int) else pl.multiple_of(left, LANES), LANES)
                row = 4 * depth + (2 * j + h) * early + top
                labels = messages[slot - 1][row : row + ROWS, left].astype(jnp.int32)
                words = look(pair[0], labels), look(pair[1], labels)
            return cell_values(words, scaled[cell, top : top + ROWS, cols], shading[cell, shaded, cols])

        parts = copy_out(result, image, sems, top, 0)
        blend_rows(
            count, depth, values, flips[here, :] == 1, result, here, lambda part, parts=parts: parts[part].start()
        )
        copies += parts
    if rows > ROWS:
        shade(rows - ROWS)
    for move in copies:
        move.wait()


def look_kernel(depth, late, lead, entries, scaled, inner, outer, known, brick, found):
    rows, width = found.shape[2:]
    pair = (entries[0], entries[1])
    for index in range(2 * depth):
        j = index % depth
        cell = j if index < depth else lead * depth + j
        for top in range(0, rows, ROWS):
            here = slice(top, top + ROWS)
            span = slice(late + top, late + top + ROWS)
            last = top + ROWS == rows
            for left in range(0, width, LANES):
                cols = slice(left, left + LANES)
                if index < depth:
                    words = known[0, j, span, cols], known[1, j, span, cols]
                else:
                    labels = brick[j, here, cols]
                    words = look(pair[0], labels), look(pair[1], labels)
                shade = outer[cell, ROWS:, cols] if last else inner[cell, late + top - ROWS : late + top, cols]
                tau, shade, colours = cell_values(words, scaled[cell, span, cols], shade)
                found[0, index, here, cols] = tau
                for c in range(3):
                    found[1 + c, index, here, cols] = shade * colours[c]


def blend_kernel(count, depth, start, late, lead, entries, flips, scaled, shading, found, *refs):
    bricks = refs[: count - 2]
    image, result, sems = refs[-3:]
    rows = result.shape[1]
    pair = (entries[0], entries[1])
    unknown = [slot for slot in range(1, count) if slot != lead]
    copies = []
    for top in range(0, rows, ROWS):
        here = slice(top, top + ROWS)
        span = slice(start + top, start + top + ROWS)
        begin = start + top - late
        inner = start + top + ROWS < scaled.shape[1]
        shaded = slice(start + top - ROWS, start + top) if inner else slice(ROWS, 2 * ROWS)

        def values(cell, cols, h, here=here, span=span, begin=begin, shaded=shaded):
            slot, j = divmod(cell, depth)
            if slot in (0, lead):
                index = j if slot == 0 else depth + j
                ready = [found[part, index, begin : begin + ROWS, cols] for part in range(4)]
                return ready[0], None, ready[1:]
            labels = bricks[unknown.index(slot)][j, here, cols]
            words = look(pair[0], labels), look(pair[1], labels)
            return cell_values(words, scaled[cell, span, cols], shading[cell, shaded, cols])

        parts = copy_out(result, image, sems, top, start)
        blend_rows(
            count, depth, values, flips[span, :] == 1, result, here, lambda part, parts=parts: parts[part].start()
        )
        copies += parts
    for move in copies:
        move.wait()


def shards(field, bins, table, march_order):
    depth, height, width = field.shape
    count = lax.axis_size("gz")
    rank = lax.axis_index("gz").astype(jnp.int32)
    rows = height // count
    total = count * depth
    half = width // 2
    slots = range(count)
    partners = sorted(range(1, count), key=lambda slot: (-slot.bit_count(), slot))
    lead, *others = partners
    params = pltpu.CompilerParams(vmem_limit_bytes=VMEM_LIMIT)

    def cost(cells):
        return pl.CostEstimate(flops=20 * cells, bytes_accessed=8 * cells, transcendentals=cells)

    done = {}
    order = {"message": lambda index: [("field", 0)], "bins": lambda index: [("message", index), "inner"]}

    def send(name, array, slot):
        index = partners.index(slot)
        waits = [done[key] for key in order.get(name, lambda index: ())(index)]
        done[name, index] = partner(after(array, *waits), "gz", slot)
        return done[name, index]

    bricks = {}
    sent = pl.pallas_call(
        functools.partial(lead_kernel, count, lead),
        out_shape=pltpu.VMEM((depth, rows, width), jnp.float32),
        in_specs=[hbm],
        out_specs=vmem,
        scratch_shapes=[pltpu.SemaphoreType.DMA],
        compiler_params=params,
        cost_estimate=cost(depth * rows * width),
        name="lead",
    )(in_hbm(field))
    bricks[lead] = send("field", sent, lead)

    *pieces, last, first = pl.pallas_call(
        functools.partial(split_kernel, count, depth, others),
        out_shape=[pltpu.VMEM((depth, rows, width), jnp.float32)] * len(others)
        + [pltpu.VMEM((depth, width), jnp.float32)] * 2,
        in_specs=[hbm],
        out_specs=[vmem] * count,
        scratch_shapes=[pltpu.VMEM((2, depth, ROWS, width), jnp.float32), pltpu.SemaphoreType.DMA((count,))],
        compiler_params=params,
        cost_estimate=cost(depth * height * width),
        name="split",
    )(in_hbm(after(field, sent)))
    for slot, sent in zip(others, pieces):
        bricks[slot] = send("field", sent, slot)

    forward = [(i, i + 1) for i in range(lax.axis_size("sy") - 1)]
    backward = [(target, origin) for origin, target in forward]
    above = lax.ppermute(last, "sy", forward)
    below = lax.ppermute(first, "sy", backward)

    early = max(rows // 2 // ROWS, 1) * ROWS
    late = rows - early
    later = []
    if late:
        later = [(0, 0, rows), (lead, early, late)]
        pieces = [(early, late - ROWS), (rows - ROWS, ROWS)] if late > ROWS else [(early, late)]
        later += [(slot, top, size) for top, size in pieces for slot in others]
    else:
        pieces = []
        later = [(0, 0, rows)]
    message_rows = 4 * depth + 2 * depth * early
    packed = pl.pallas_call(
        functools.partial(pack_kernel, count, depth, early, later),
        out_shape=[pltpu.VMEM((message_rows, half), jnp.float32)] * (count - 1)
        + [
            jax.ShapeDtypeStruct((4 * depth, half), jnp.float32),
            jax.ShapeDtypeStruct((2, ROWS, table.shape[1]), jnp.int32),
            jax.ShapeDtypeStruct((rows, LANES), jnp.int32),
        ]
        + [jax.ShapeDtypeStruct((depth, size, width), jnp.int32) for _, _, size in later],
        in_specs=[vmem, vmem, vmem, pl.BlockSpec(memory_space=pltpu.SMEM), hbm, hbm],
        out_specs=[vmem] * (count + 2 + len(later)),
        scratch_shapes=[
            pltpu.VMEM((count, depth, ROWS, width), jnp.float32),
            pltpu.VMEM((count, depth, ROWS, width), jnp.float32),
            pltpu.VMEM((count - 1, depth, early, width), jnp.int32),
            pltpu.SemaphoreType.DMA((count, 3)),
            pltpu.SemaphoreType.DMA((len(later),)),
        ],
        compiler_params=params,
        cost_estimate=cost(depth * height * width),
        name="pack",
    )(above, below, table.astype(jnp.float32), march_order, in_hbm(field), in_hbm(bins))
    messages = {}
    for slot in partners:
        messages[slot] = send("message", packed[slot - 1], slot)
    edges, entries, flips = packed[count - 1 : count + 2]
    cuts = packed[count + 2 :]

    slab = pl.pallas_call(
        functools.partial(side_kernel, count, depth),
        out_shape=pltpu.VMEM((total, rows, LANES), jnp.float32),
        in_specs=[hbm] + [vmem] * (count - 1),
        out_specs=vmem,
        scratch_shapes=[pltpu.VMEM((depth, rows, LANES), jnp.float32), pltpu.SemaphoreType.DMA],
        compiler_params=params,
        cost_estimate=cost(total * rows * LANES),
        name="side",
    )(in_hbm(field), *[bricks[slot] for slot in slots[1:]])
    beside = partner(slab, "sx", 1)

    ext, scaled, inner, known, token = pl.pallas_call(
        functools.partial(inner_kernel, count, depth),
        out_shape=(
            pltpu.VMEM((total + 2, rows + 2 * ROWS, width + 2 * LANES), jnp.float32),
            pltpu.VMEM((total, rows, width), jnp.float32),
            pltpu.VMEM((total, max(rows - 2 * ROWS, ROWS), width), jnp.float32),
            pltpu.VMEM((2, depth, rows, width), jnp.int32),
            jax.ShapeDtypeStruct((ROWS, LANES), jnp.float32),
        ),
        in_specs=[hbm] + [vmem] * (count + 4),
        out_specs=[vmem] * 5,
        scratch_shapes=[pltpu.VMEM((depth, rows, width), jnp.float32), pltpu.SemaphoreType.DMA],
        compiler_params=params,
        cost_estimate=cost(total * rows * width),
        name="inner",
    )(in_hbm(field), edges, beside, entries, flips, *[bricks[slot] for slot in slots[1:]], cuts[0])
    done["inner"] = token

    image_shape = jax.ShapeDtypeStruct((4, rows, width), jnp.float32)
    outer, image = pl.pallas_call(
        functools.partial(outer_kernel, count, depth),
        out_shape=(pltpu.VMEM((total, 2 * ROWS, width), jnp.float32), image_shape),
        in_specs=[vmem] * (count + 5),
        out_specs=(vmem, hbm),
        scratch_shapes=[
            pltpu.VMEM((4, early, width), jnp.float32),
            pltpu.SemaphoreType.DMA((early // ROWS, COPIES)),
        ],
        compiler_params=params,
        cost_estimate=cost(total * rows * width),
        name="outer",
    )(entries, flips, ext, scaled, inner, known, *[messages[slot] for slot in slots[1:]])
    if not late:
        return image

    arrived = [send("bins", cut, slot) for (slot, _, _), cut in zip(later[1:], cuts[1:])]
    found = pl.pallas_call(
        functools.partial(look_kernel, depth, early, lead),
        out_shape=pltpu.VMEM((4, 2 * depth, late, width), jnp.float32),
        in_specs=[vmem] * 6,
        out_specs=vmem,
        compiler_params=params,
        cost_estimate=cost(depth * late * width),
        name="look",
    )(entries, scaled, inner, outer, known, arrived[0])
    for index, (top, size) in enumerate(pieces):
        labels = arrived[1 + index * len(others) : 1 + (index + 1) * len(others)]
        labels = [labels[others.index(slot)] for slot in sorted(others)]
        shading = outer if top + size == rows else inner
        operands = [entries, flips, scaled, shading, found, *labels, image]
        image = pl.pallas_call(
            functools.partial(blend_kernel, count, depth, top, early, lead),
            out_shape=image_shape,
            in_specs=[vmem] * (len(operands) - 1) + [hbm],
            out_specs=hbm,
            scratch_shapes=[
                pltpu.VMEM((4, size, width), jnp.float32),
                pltpu.SemaphoreType.DMA((size // ROWS, COPIES)),
            ],
            input_output_aliases={len(operands) - 1: 0},
            compiler_params=params,
            cost_estimate=cost(total * size * width),
            name="blend",
        )(*operands)
    return image


def solution(mesh):
    placed = (P("gz", "sy", "sx"), P("gz", "sy", "sx"), P(), P("sy"))
    return jax.shard_map(
        shards, mesh=mesh, in_specs=placed, out_specs=P(None, ("sy", "gz"), "sx"), check_vma=False
    )
```

```python
import functools

import jax
import jax.numpy as jnp
from jax import lax
from jax.experimental import pallas as pl
from jax.experimental.pallas import tpu as pltpu
from jax.sharding import PartitionSpec as P

light_x = 0.36
light_y = 0.48
light_z = 0.8
LANES = 128
ROWS = 8
COLOUR_UNIT = 2.0**-12
OPACITY_UNIT = 2.0**-13
HALF_WORD = 16
LOG2_E = 1.4426950408889634
UNROLLED = 32
COPIES = 4
VMEM_LIMIT = 40 * 1024 * 1024

vmem = pl.BlockSpec(memory_space=pltpu.VMEM)
hbm = pl.BlockSpec(memory_space=pltpu.HBM)


def partner(x, axis, distance):
    return lax.ppermute(x, axis, [(i, i ^ distance) for i in range(lax.axis_size(axis))])


def in_hbm(array):
    return pltpu.with_memory_space_constraint(array, pltpu.HBM)


def after(array, *others):
    return lax.optimization_barrier((array, *others))[0]


def run_copies(moves):
    for move in moves:
        move.start()
    for move in moves:
        move.wait()


def lead_kernel(count, slot, field, piece, sem):
    rows = piece.shape[1]
    start = pl.multiple_of((lax.axis_index("gz") ^ slot) * rows, ROWS)
    run_copies([pltpu.make_async_copy(field.at[:, pl.ds(start, rows)], piece, sem)])


def split_kernel(count, depth, slots, field, *refs):
    pieces = refs[: len(slots)]
    last, first, ends, sems = refs[len(slots) :]
    height = field.shape[1]
    rows = height // count
    rank = lax.axis_index("gz")
    moves = [
        pltpu.make_async_copy(field.at[:, height - ROWS :], ends.at[0], sems.at[0]),
        pltpu.make_async_copy(field.at[:, :ROWS], ends.at[1], sems.at[1]),
    ]
    for index, slot in enumerate(slots):
        start = pl.multiple_of((rank ^ slot) * rows, ROWS)
        moves.append(pltpu.make_async_copy(field.at[:, pl.ds(start, rows)], pieces[index], sems.at[2 + index]))
    run_copies(moves)
    for j in range(depth):
        last[j : j + 1, :] = ends[0, j, ROWS - 1 :, :]
        first[j : j + 1, :] = ends[1, j, :1, :]


def pack_kernel(count, depth, early, later, above, below, table, march, field, bins, *refs):
    messages = refs[: count - 1]
    edges, entries, flips, *pieces, high, low, labels, sems, cut_sems = refs[count - 1 :]
    height, width = field.shape[1:]
    rows = height // count
    half = width // 2
    rank = lax.axis_index("gz")
    copies = []
    for slot in range(count):
        target = rank ^ slot
        top = pl.multiple_of(jnp.maximum(target * rows - ROWS, 0), ROWS)
        bottom = pl.multiple_of(jnp.minimum(target * rows + rows, height - ROWS), ROWS)
        start = pl.multiple_of(target * rows, ROWS)
        moves = [
            pltpu.make_async_copy(field.at[:, pl.ds(top, ROWS)], high.at[slot], sems.at[slot, 0]),
            pltpu.make_async_copy(field.at[:, pl.ds(bottom, ROWS)], low.at[slot], sems.at[slot, 1]),
        ]
        if slot:
            moves.append(
                pltpu.make_async_copy(bins.at[:, pl.ds(start, early)], labels.at[slot - 1], sems.at[slot, 2])
            )
        for move in moves:
            move.start()
        copies.append(moves)
    cuts = []
    for index, (slot, top, size) in enumerate(later):
        start = pl.multiple_of((rank ^ slot) * rows + top, ROWS)
        cuts.append(pltpu.make_async_copy(bins.at[:, pl.ds(start, size)], pieces[index], cut_sems.at[index]))
        cuts[-1].start()
    pair = pack_entries(table)
    for word in range(2):
        entries[word] = pair[word]
    for row in range(rows):
        flips[row : row + 1, :] = jnp.full((1, LANES), march[rank * rows + row], jnp.int32)
    for slot in range(count):
        target = rank ^ slot
        for move in copies[slot]:
            move.wait()
        message = messages[slot - 1] if slot else edges
        for j in range(depth):
            upper = jnp.where(target == 0, above[j : j + 1, :], high[slot, j, ROWS - 1 : ROWS, :])
            lower = jnp.where(target == count - 1, below[j : j + 1, :], low[slot, j, 0:1, :])
            for h in range(2):
                cols = slice(h * half, (h + 1) * half)
                at = 2 * depth * h + j
                message[at : at + 1, :] = upper[:, cols]
                message[at + depth : at + depth + 1, :] = lower[:, cols]
                if slot:
                    first = 4 * depth + (2 * j + h) * early
                    message[first : first + early, :] = labels[slot - 1, j, :, cols].astype(jnp.float32)
    for move in cuts:
        move.wait()


def side_kernel(count, depth, field, *refs):
    bricks = (None,) + refs[: count - 1]
    slab, own, sem = refs[count - 1 :]
    rows = slab.shape[1]
    width = field.shape[2]
    side = lax.axis_index("sx")
    start = pl.multiple_of(lax.axis_index("gz") * rows, ROWS)
    column = pl.multiple_of((1 - side) * (width - LANES), LANES)
    move = pltpu.make_async_copy(field.at[:, pl.ds(start, rows), pl.ds(column, LANES)], own, sem)
    move.start()
    for slot in range(1, count):
        for j in range(depth):
            slab[slot * depth + j] = jnp.where(
                side == 1, bricks[slot][j, :, :LANES], bricks[slot][j, :, width - LANES :]
            )
    move.wait()
    for j in range(depth):
        slab[j] = own[j]


def pack_entries(table):
    units = [1.0 / COLOUR_UNIT] * 3 + [1.0 / OPACITY_UNIT]
    rows = [
        jnp.broadcast_to((table[c : c + 1, :] * units[c]).astype(jnp.int32), (ROWS, table.shape[1])) for c in range(4)
    ]
    return rows[0] | rows[1] << HALF_WORD, rows[2] | rows[3] << HALF_WORD


def look(entries, labels):
    return jnp.take_along_axis(entries, labels, axis=1, mode="promise_in_bounds")


def low_part(words):
    return (words & ((1 << HALF_WORD) - 1)).astype(jnp.float32)


def high_part(words):
    return (words >> HALF_WORD).astype(jnp.float32)


def in_front(sums, bit):
    if len(sums) == 1:
        return [None], sums[0]
    middle = len(sums) // 2
    low, low_sum = in_front(sums[:middle], bit - 1)
    high, high_sum = in_front(sums[middle:], bit - 1)
    swapped = jnp.where(lax.axis_index("gz") >> bit & 1 == 1, 1.0, 0.0)
    low_adds = high_sum * swapped
    high_adds = low_sum * (1.0 - swapped)
    fronts = [low_adds if front is None else front + low_adds for front in low]
    fronts += [high_adds if front is None else front + high_adds for front in high]
    return fronts, low_sum + high_sum


def cell_values(words, scaled, shade):
    return high_part(words[1]) * scaled, shade, (low_part(words[0]), high_part(words[0]), low_part(words[1]))


def blend_rows(count, depth, values, back, result, here, finish):
    tiles = result.shape[2] // LANES
    unroll = max(min(tiles // COPIES, UNROLLED // (count * depth)), 1)

    def blend_tile(cols, h):
        cells = [values(cell, cols, h) for cell in range(count * depth)]
        inner = []
        for slot in range(count):
            sums = [cells[slot * depth][0]]
            for j in range(1, depth):
                sums.append(sums[-1] + cells[slot * depth + j][0])
            inner.append(sums)
        fronts, whole = in_front([sums[-1] for sums in inner], count.bit_length() - 2)
        shift = jnp.where(back, -whole, 0.0)
        colour = [jnp.zeros((ROWS, LANES), jnp.float32) for _ in range(3)]
        for slot in range(count):
            base = fronts[slot] + shift
            through = [jnp.exp2(base)] + [jnp.exp2(base + part) for part in inner[slot]]
            for j in range(depth):
                _, shade, colours = cells[slot * depth + j]
                weight = jnp.abs(through[j] - through[j + 1])
                if shade is not None:
                    weight = weight * shade
                colour = [total + weight * part for total, part in zip(colour, colours)]
        for c in range(3):
            result[c, here, cols] = colour[c]
        result[3, here, cols] = 1.0 - jnp.exp2(-jnp.abs(whole))

    quarter = tiles // COPIES
    for part in range(COPIES):
        h = 2 * part // COPIES
        if unroll == quarter:
            for tile in range(part * quarter, (part + 1) * quarter):
                blend_tile(slice(tile * LANES, (tile + 1) * LANES), h)
        else:

            def tile_step(step, _, part=part, h=h):
                for tile in range(unroll):
                    left = (part * quarter + step * unroll + tile) * LANES
                    blend_tile(pl.ds(pl.multiple_of(left, LANES), LANES), h)
                return 0

            lax.fori_loop(0, quarter // unroll, tile_step, 0)
        finish(part)


def copy_out(result, image, sems, top, start):
    columns = result.shape[2] // COPIES
    return [
        pltpu.make_async_copy(
            result.at[:, top : top + ROWS, part * columns : (part + 1) * columns],
            image.at[:, start + top : start + top + ROWS, part * columns : (part + 1) * columns],
            sems.at[top // ROWS, part],
        )
        for part in range(COPIES)
    ]


def shade_tile(ext, at, top, width, dy_of, store):
    here = slice(ROWS + top, 2 * ROWS + top)
    lane = lax.broadcasted_iota(jnp.int32, (ROWS, LANES), 1)
    first = lane == 0
    last = lane == LANES - 1
    tiles = [ext[at + 1, here, left : left + LANES] for left in range(0, width + 2 * LANES, LANES)]
    toward = [pltpu.roll(tile, LANES - 1, 1) for tile in tiles]
    away = [pltpu.roll(tile, 1, 1) for tile in tiles]
    for c in range(1, width // LANES + 1):
        cols = slice(c * LANES, (c + 1) * LANES)
        dx = jnp.where(last, toward[c + 1], toward[c]) - jnp.where(first, away[c - 1], away[c])
        dy = dy_of(
            c - 1,
            ext[at + 1, ROWS + top + 1 : 2 * ROWS + top + 1, cols]
            - ext[at + 1, ROWS + top - 1 : 2 * ROWS + top - 1, cols],
        )
        dz = ext[at + 2, here, cols] - ext[at, here, cols]
        facing = jnp.abs((0.5 * light_x) * dx + (0.5 * light_y) * dy + (0.5 * light_z) * dz)
        square = 0.25 * (dx * dx + dy * dy + dz * dz) + 1.0
        store(c - 1, 0.3 * COLOUR_UNIT + (0.7 * COLOUR_UNIT) * facing * lax.rsqrt(square))


def inner_kernel(count, depth, field, edges, beside, entries, flips, *refs):
    parts = len(refs) - (count - 1) - 7
    bricks = refs[: count - 1]
    own_bins = refs[count - 1 : count - 1 + parts]
    ext, scaled, inner, known, token, own_brick, sem = refs[count - 1 + parts :]
    rows, width = scaled.shape[1:]
    half = width // 2
    total = count * depth
    rank = lax.axis_index("gz")
    side = lax.axis_index("sx")
    inside = slice(ROWS, ROWS + rows)
    move = pltpu.make_async_copy(field.at[:, pl.ds(pl.multiple_of(rank * rows, ROWS), rows)], own_brick, sem)
    move.start()
    bricks = (own_brick, *bricks)
    unit = jnp.where(flips[...] == 1, OPACITY_UNIT * LOG2_E, -OPACITY_UNIT * LOG2_E)
    zero_plane = jnp.zeros((rows, width), jnp.float32)
    zero_row = jnp.zeros((ROWS, width), jnp.float32)
    ext[0, inside, LANES : LANES + width] = zero_plane
    ext[total + 1, inside, LANES : LANES + width] = zero_plane
    for slot in reversed(range(count)):
        if slot == 0:
            move.wait()
        for j in range(depth):
            at = (rank ^ slot) * depth + j
            plane = bricks[slot][j]
            for left in range(0, width, LANES):
                cols = slice(left, left + LANES)
                scaled[slot * depth + j, :, cols] = bricks[slot][j, :, cols] * unit
            ext[at + 1, inside, LANES : LANES + width] = plane
            ext[at + 1, :ROWS, LANES : LANES + width] = zero_row
            ext[at + 1, ROWS + rows :, LANES : LANES + width] = zero_row
            if slot == 0:
                for h in range(2):
                    cols = slice(LANES + h * half, LANES + (h + 1) * half)
                    row = 2 * depth * h + j
                    ext[at + 1, ROWS - 1 : ROWS, cols] = edges[row : row + 1, :]
                    ext[at + 1, ROWS + rows : ROWS + rows + 1, cols] = edges[row + depth : row + depth + 1, :]
            column = beside[slot * depth + j]
            ext[at + 1, inside, :LANES] = jnp.where(side == 1, column, 0.0)
            ext[at + 1, inside, LANES + width :] = jnp.where(side == 0, column, 0.0)
    pair = (entries[0], entries[1])
    start = 0
    for part in own_bins:
        size = part.shape[1]
        for j in range(depth):
            for top in range(0, size, ROWS):
                for left in range(0, width, LANES):
                    cols = slice(left, left + LANES)
                    labels = part[j, top : top + ROWS, cols]
                    for word in range(2):
                        known[word, j, start + top : start + top + ROWS, cols] = look(pair[word], labels)
        start += size

    def plane_step(cell, _):
        at = (rank ^ (cell // depth)) * depth + cell % depth
        for top in range(ROWS, rows - ROWS, ROWS):

            def store(c, value, top=top):
                inner[cell, top - ROWS : top, c * LANES : (c + 1) * LANES] = value

            shade_tile(ext, at, top, width, lambda c, dy: dy, store)
        return 0

    if rows > 2 * ROWS:
        lax.fori_loop(0, total, plane_step, 0)
    else:
        inner[...] = jnp.zeros_like(inner)
    token[...] = jnp.zeros_like(token)


def outer_kernel(count, depth, entries, flips, ext, scaled, inner, known, *refs):
    messages = refs[: count - 1]
    outer, image, result, sems = refs[count - 1 :]
    rows, width = scaled.shape[1:]
    early = result.shape[1]
    half = width // 2
    rank = lax.axis_index("gz")
    pair = (entries[0], entries[1])
    row_of = lax.broadcasted_iota(jnp.int32, (ROWS, LANES), 0)

    def shade(top):
        for cell in range(count * depth):
            slot, j = divmod(cell, depth)
            at = (rank ^ slot) * depth + j

            def dy_of(c, dy, slot=slot, j=j):
                if slot == 0:
                    return dy
                h, left = c * LANES // half, c * LANES % half
                row = 2 * depth * h + j
                cols = slice(left, left + LANES)
                if top == 0:
                    dy = dy - jnp.where(row_of == 0, messages[slot - 1][row : row + 1, cols], 0.0)
                if top == rows - ROWS:
                    beyond = messages[slot - 1][row + depth : row + depth + 1, cols]
                    dy = dy + jnp.where(row_of == ROWS - 1, beyond, 0.0)
                return dy

            def store(c, value, cell=cell):
                place = 0 if top == 0 else ROWS
                outer[cell, place : place + ROWS, c * LANES : (c + 1) * LANES] = value

            shade_tile(ext, at, top, width, dy_of, store)

    shade(0)
    copies = []
    for top in range(0, early, ROWS):
        here = slice(top, top + ROWS)

        shading, shaded = (outer, slice(0, ROWS)) if top == 0 else (inner, slice(top - ROWS, top))

        def values(cell, cols, h, top=top, shading=shading, shaded=shaded):
            slot, j = divmod(cell, depth)
            if slot == 0:
                words = tuple(known[word, j, top : top + ROWS, cols] for word in range(2))
            else:
                left = cols.start - h * half
                left = pl.ds(left if isinstance(left, int) else pl.multiple_of(left, LANES), LANES)
                row = 4 * depth + (2 * j + h) * early + top
                labels = messages[slot - 1][row : row + ROWS, left].astype(jnp.int32)
                words = look(pair[0], labels), look(pair[1], labels)
            return cell_values(words, scaled[cell, top : top + ROWS, cols], shading[cell, shaded, cols])

        parts = copy_out(result, image, sems, top, 0)
        blend_rows(
            count, depth, values, flips[here, :] == 1, result, here, lambda part, parts=parts: parts[part].start()
        )
        copies += parts
    if rows > ROWS:
        shade(rows - ROWS)
    for move in copies:
        move.wait()


def look_kernel(depth, late, lead, entries, scaled, inner, outer, known, brick, found):
    rows, width = found.shape[2:]
    pair = (entries[0], entries[1])
    for index in range(2 * depth):
        j = index % depth
        cell = j if index < depth else lead * depth + j
        for top in range(0, rows, ROWS):
            here = slice(top, top + ROWS)
            span = slice(late + top, late + top + ROWS)
            last = top + ROWS == rows
            for left in range(0, width, LANES):
                cols = slice(left, left + LANES)
                if index < depth:
                    words = known[0, j, span, cols], known[1, j, span, cols]
                else:
                    labels = brick[j, here, cols]
                    words = look(pair[0], labels), look(pair[1], labels)
                shade = outer[cell, ROWS:, cols] if last else inner[cell, late + top - ROWS : late + top, cols]
                tau, shade, colours = cell_values(words, scaled[cell, span, cols], shade)
                found[0, index, here, cols] = tau
                for c in range(3):
                    found[1 + c, index, here, cols] = shade * colours[c]


def blend_kernel(count, depth, start, late, lead, entries, flips, scaled, shading, found, *refs):
    bricks = refs[: count - 2]
    image, result, sems = refs[-3:]
    rows = result.shape[1]
    pair = (entries[0], entries[1])
    unknown = [slot for slot in range(1, count) if slot != lead]
    copies = []
    for top in range(0, rows, ROWS):
        here = slice(top, top + ROWS)
        span = slice(start + top, start + top + ROWS)
        begin = start + top - late
        inner = start + top + ROWS < scaled.shape[1]
        shaded = slice(start + top - ROWS, start + top) if inner else slice(ROWS, 2 * ROWS)

        def values(cell, cols, h, here=here, span=span, begin=begin, shaded=shaded):
            slot, j = divmod(cell, depth)
            if slot in (0, lead):
                index = j if slot == 0 else depth + j
                ready = [found[part, index, begin : begin + ROWS, cols] for part in range(4)]
                return ready[0], None, ready[1:]
            labels = bricks[unknown.index(slot)][j, here, cols]
            words = look(pair[0], labels), look(pair[1], labels)
            return cell_values(words, scaled[cell, span, cols], shading[cell, shaded, cols])

        parts = copy_out(result, image, sems, top, start)
        blend_rows(
            count, depth, values, flips[span, :] == 1, result, here, lambda part, parts=parts: parts[part].start()
        )
        copies += parts
    for move in copies:
        move.wait()


def shards(field, bins, table, march_order):
    depth, height, width = field.shape
    count = lax.axis_size("gz")
    rank = lax.axis_index("gz").astype(jnp.int32)
    rows = height // count
    total = count * depth
    half = width // 2
    slots = range(count)
    partners = sorted(range(1, count), key=lambda slot: (-slot.bit_count(), slot))
    lead, *others = partners
    params = pltpu.CompilerParams(vmem_limit_bytes=VMEM_LIMIT)

    def cost(cells):
        return pl.CostEstimate(flops=20 * cells, bytes_accessed=8 * cells, transcendentals=cells)

    done = {}
    order = {
        "message": lambda index: [("field", 0)],
        "bins": lambda index: [("message", index), "inner"] if index else [("message", 0), "beside"],
    }

    def send(name, array, slot):
        index = partners.index(slot)
        waits = [done[key] for key in order.get(name, lambda index: ())(index)]
        done[name, index] = partner(after(array, *waits), "gz", slot)
        return done[name, index]

    bricks = {}
    sent = pl.pallas_call(
        functools.partial(lead_kernel, count, lead),
        out_shape=pltpu.VMEM((depth, rows, width), jnp.float32),
        in_specs=[hbm],
        out_specs=vmem,
        scratch_shapes=[pltpu.SemaphoreType.DMA],
        compiler_params=params,
        cost_estimate=cost(depth * rows * width),
        name="lead",
    )(in_hbm(field))
    bricks[lead] = send("field", sent, lead)

    *pieces, last, first = pl.pallas_call(
        functools.partial(split_kernel, count, depth, others),
        out_shape=[pltpu.VMEM((depth, rows, width), jnp.float32)] * len(others)
        + [pltpu.VMEM((depth, width), jnp.float32)] * 2,
        in_specs=[hbm],
        out_specs=[vmem] * count,
        scratch_shapes=[pltpu.VMEM((2, depth, ROWS, width), jnp.float32), pltpu.SemaphoreType.DMA((count,))],
        compiler_params=params,
        cost_estimate=cost(depth * height * width),
        name="split",
    )(in_hbm(after(field, sent)))
    for slot, sent in zip(others, pieces):
        bricks[slot] = send("field", sent, slot)

    forward = [(i, i + 1) for i in range(lax.axis_size("sy") - 1)]
    backward = [(target, origin) for origin, target in forward]
    above = lax.ppermute(last, "sy", forward)
    below = lax.ppermute(first, "sy", backward)

    early = max(rows // 2 // ROWS, 1) * ROWS
    late = rows - early
    later = []
    if late:
        later = [(0, 0, rows), (lead, early, late)]
        pieces = [(early, late - ROWS), (rows - ROWS, ROWS)] if late > ROWS else [(early, late)]
        later += [(slot, top, size) for top, size in pieces for slot in others]
    else:
        pieces = []
        later = [(0, 0, rows)]
    message_rows = 4 * depth + 2 * depth * early
    packed = pl.pallas_call(
        functools.partial(pack_kernel, count, depth, early, later),
        out_shape=[pltpu.VMEM((message_rows, half), jnp.float32)] * (count - 1)
        + [
            jax.ShapeDtypeStruct((4 * depth, half), jnp.float32),
            jax.ShapeDtypeStruct((2, ROWS, table.shape[1]), jnp.int32),
            jax.ShapeDtypeStruct((rows, LANES), jnp.int32),
        ]
        + [jax.ShapeDtypeStruct((depth, size, width), jnp.int32) for _, _, size in later],
        in_specs=[vmem, vmem, vmem, pl.BlockSpec(memory_space=pltpu.SMEM), hbm, hbm],
        out_specs=[vmem] * (count + 2 + len(later)),
        scratch_shapes=[
            pltpu.VMEM((count, depth, ROWS, width), jnp.float32),
            pltpu.VMEM((count, depth, ROWS, width), jnp.float32),
            pltpu.VMEM((count - 1, depth, early, width), jnp.int32),
            pltpu.SemaphoreType.DMA((count, 3)),
            pltpu.SemaphoreType.DMA((len(later),)),
        ],
        compiler_params=params,
        cost_estimate=cost(depth * height * width),
        name="pack",
    )(above, below, table.astype(jnp.float32), march_order, in_hbm(field), in_hbm(bins))
    messages = {}
    for slot in partners:
        messages[slot] = send("message", packed[slot - 1], slot)
    edges, entries, flips = packed[count - 1 : count + 2]
    cuts = packed[count + 2 :]

    slab = pl.pallas_call(
        functools.partial(side_kernel, count, depth),
        out_shape=pltpu.VMEM((total, rows, LANES), jnp.float32),
        in_specs=[hbm] + [vmem] * (count - 1),
        out_specs=vmem,
        scratch_shapes=[pltpu.VMEM((depth, rows, LANES), jnp.float32), pltpu.SemaphoreType.DMA],
        compiler_params=params,
        cost_estimate=cost(total * rows * LANES),
        name="side",
    )(in_hbm(field), *[bricks[slot] for slot in slots[1:]])
    beside = partner(slab, "sx", 1)
    done["beside"] = beside

    ext, scaled, inner, known, token = pl.pallas_call(
        functools.partial(inner_kernel, count, depth),
        out_shape=(
            pltpu.VMEM((total + 2, rows + 2 * ROWS, width + 2 * LANES), jnp.float32),
            pltpu.VMEM((total, rows, width), jnp.float32),
            pltpu.VMEM((total, max(rows - 2 * ROWS, ROWS), width), jnp.float32),
            pltpu.VMEM((2, depth, rows, width), jnp.int32),
            jax.ShapeDtypeStruct((ROWS, LANES), jnp.float32),
        ),
        in_specs=[hbm] + [vmem] * (count + 4),
        out_specs=[vmem] * 5,
        scratch_shapes=[pltpu.VMEM((depth, rows, width), jnp.float32), pltpu.SemaphoreType.DMA],
        compiler_params=params,
        cost_estimate=cost(total * rows * width),
        name="inner",
    )(in_hbm(field), edges, beside, entries, flips, *[bricks[slot] for slot in slots[1:]], cuts[0])
    done["inner"] = token

    image_shape = jax.ShapeDtypeStruct((4, rows, width), jnp.float32)
    outer, image = pl.pallas_call(
        functools.partial(outer_kernel, count, depth),
        out_shape=(pltpu.VMEM((total, 2 * ROWS, width), jnp.float32), image_shape),
        in_specs=[vmem] * (count + 5),
        out_specs=(vmem, hbm),
        scratch_shapes=[
            pltpu.VMEM((4, early, width), jnp.float32),
            pltpu.SemaphoreType.DMA((early // ROWS, COPIES)),
        ],
        compiler_params=params,
        cost_estimate=cost(total * rows * width),
        name="outer",
    )(entries, flips, ext, scaled, inner, known, *[messages[slot] for slot in slots[1:]])
    if not late:
        return image

    arrived = [send("bins", cut, slot) for (slot, _, _), cut in zip(later[1:], cuts[1:])]
    found = pl.pallas_call(
        functools.partial(look_kernel, depth, early, lead),
        out_shape=pltpu.VMEM((4, 2 * depth, late, width), jnp.float32),
        in_specs=[vmem] * 6,
        out_specs=vmem,
        compiler_params=params,
        cost_estimate=cost(depth * late * width),
        name="look",
    )(entries, scaled, inner, outer, known, arrived[0])
    for index, (top, size) in enumerate(pieces):
        labels = arrived[1 + index * len(others) : 1 + (index + 1) * len(others)]
        labels = [labels[others.index(slot)] for slot in sorted(others)]
        shading = outer if top + size == rows else inner
        operands = [entries, flips, scaled, shading, found, *labels, image]
        image = pl.pallas_call(
            functools.partial(blend_kernel, count, depth, top, early, lead),
            out_shape=image_shape,
            in_specs=[vmem] * (len(operands) - 1) + [hbm],
            out_specs=hbm,
            scratch_shapes=[
                pltpu.VMEM((4, size, width), jnp.float32),
                pltpu.SemaphoreType.DMA((size // ROWS, COPIES)),
            ],
            input_output_aliases={len(operands) - 1: 0},
            compiler_params=params,
            cost_estimate=cost(total * size * width),
            name="blend",
        )(*operands)
    return image


def solution(mesh):
    placed = (P("gz", "sy", "sx"), P("gz", "sy", "sx"), P(), P("sy"))
    return jax.shard_map(
        shards, mesh=mesh, in_specs=placed, out_specs=P(None, ("sy", "gz"), "sx"), check_vma=False
    )
```
